512 devices in a mesh: dp: 64 (over x, z_lo, core), tensor: 8 (over y, z_hi).
Axes of the slice: x: 4, y: 4, z: 16 (z_hi: 2, z_lo: 8; z = z_hi * 8 + z_lo), core: 2. Of those that a mesh axis runs over, the one named last changes fastest.
Arguments:
- hidden: bfloat16 [16384, 4096], P('dp', 'tensor'), may hold values from -12 to 12
- targets: int32 [16384], P('dp'), may hold values from 0 to 8191
- lengths: int32 [64], P('dp'), may hold values from 64 to 256
- layer_gain: float32 [2, 4096], P(None, 'tensor'), may hold values from 0.25 to 1.75
- down_codes: bfloat16 [2, 4096, 512], P(None, ('tensor', 'dp')), may hold values from -4 to 4
- down_scales: float32 [2, 32, 4], P(None, 'tensor'), may hold values from 0.0078125 to 0.03125
- up_codes: bfloat16 [2, 512, 4096], P(None, None, ('tensor', 'dp')), may hold values from -4 to 4
- up_scales: float32 [2, 4, 32], P(None, None, 'tensor'), may hold values from 0.022097087 to 0.088388346
- final_gain: float32 [4096], replicated, may hold values from 0.25 to 1.75
- head_codes: bfloat16 [4096, 8192], P('dp', 'tensor'), may hold values from -4 to 4
- head_scales: float32 [32, 64], P(None, 'tensor'), may hold values from 0.03125 to 2, as said below
Outputs:
- log_probs: float32 [16384], P('dp')
The draws below stay inside these ranges and needn't reach their ends.
Inputs may be any that keep to these rules, and one draw needn't show every extreme that they name: `head_scales`: positive block scales of the output projection.
All inputs are finite; a program needn't handle non-finite values.
Results may differ from the reference program's by a relative error of at most 0.008.
Values may be sent and summed in bfloat16 or wider, within the bound.
No kernel may reach another device: no remote copies, remote signals or barrier semaphores. Data moves between devices by JAX's collectives and lax.ppermute only.
A program may use at most 64 MiB of HBM per device.

```python
import math
import jax
import jax.numpy as jnp
import numpy as np
from jax import lax

D = 4096
R = 512
V = 8192
L = 2
TOK_DEV = 256
TOKENS = 16384
SEQS = 64
N_DP = 64
N_TENSOR = 8


def column_scaled(key, low_scale, high_scale, entries):
    column = jnp.arange(D, dtype=jnp.float32) / D
    scale = jnp.exp(jnp.log(low_scale) + column * (jnp.log(high_scale) - jnp.log(low_scale)))
    return entries * scale[None, :]


def draw_hidden(key, part):
    key = jax.random.fold_in(key, 5)
    entries = jnp.clip(jax.random.normal(key, (TOKENS, D), jnp.float32), -4.0, 4.0)
    values = column_scaled(key, 0.5, 2.0, entries)
    return values.astype(jnp.bfloat16)


def draw_head_scales(key, part):
    key = jax.random.fold_in(key, 11)
    uniform_part = jax.random.uniform(key, (D // 128, V // 128), jnp.float32)
    lower_log = jnp.log(2.0 * D ** (-0.5))
    upper_log = jnp.log(5.0 * D ** (-0.5))
    return jnp.exp(lower_log + uniform_part * (upper_log - lower_log))


def touch_ends(values, rng, low, largest):
    place = [jax.random.randint(jax.random.fold_in(rng, axis), (), 0, length) for axis, length in enumerate(values.shape)]
    longest = values.shape.index(max(values.shape))
    beside = place[:longest] + [(place[longest] + 1) % values.shape[longest]] + place[longest + 1:]
    return values.at[tuple(place)].set(low).at[tuple(beside)].set(largest)


def level_of(rng, extent, pieces, smallest, largest):
    loudness = 1.0
    for axis_at, shards_of in pieces:
        steps = jax.random.uniform(jax.random.fold_in(jax.random.fold_in(rng, 6), axis_at), (shards_of,), jnp.float32, smallest / len(pieces), largest / len(pieces))
        loudness = loudness * jnp.repeat(jnp.exp(steps), extent[axis_at] // shards_of).reshape((-1,) + (1,) * (len(extent) - 1 - axis_at))
    return loudness


def rank_table(number_of, slope):
    loads = [(1 << 20) // math.isqrt(standing ** slope) + 1 for standing in range(1, number_of + 1)]
    width = 1 + sum(loads) // (1 << 30)
    return np.cumsum(np.array([max(1, weight // width) for weight in loads]))


def ranked(own_key, extent, number_of, lean):
    grid = rank_table(number_of, lean)
    pick = jax.random.randint(jax.random.fold_in(own_key, 1), extent, 0, int(grid[number_of - 1]))
    grade = jnp.searchsorted(jnp.asarray(grid, jnp.int32), pick, side="right")
    return jax.random.permutation(jax.random.fold_in(own_key, 2), number_of)[grade].astype(jnp.int32)


def scatter_about(rng, dims, width, limit, cuts=(), kind=jnp.bfloat16):
    result = width * jax.random.normal(rng, dims, jnp.float32)
    if cuts:
        result = result * level_of(rng, dims, cuts, -0.22, 0.18)
    return jnp.clip(result, -limit, limit).astype(kind)


def setup_inputs(seed: int = 0) -> dict:
    streams_of = jax.random.split(jax.random.key(seed), 12)
    return {
        "hidden": draw_hidden(jax.random.fold_in(streams_of[11], 71), 0),
        "targets": touch_ends(ranked(streams_of[1], (TOKENS,), V, 2), jax.random.fold_in(streams_of[1], 3), 0, V - 1).astype(jnp.int32),
        "lengths": touch_ends(jax.random.randint(streams_of[2], (SEQS,), TOK_DEV // 4, TOK_DEV + 1), jax.random.fold_in(streams_of[2], 1), TOK_DEV // 4, TOK_DEV).astype(jnp.int32),
        "layer_gain": jnp.clip(1.0 + 0.15 * jax.random.normal(streams_of[3], (L, D), jnp.float32), 0.25, 1.75),
        "down_codes": scatter_about(streams_of[4], (L, D, R), 1.0, 4.0, ((1, 512),)),
        "down_scales": jnp.clip(jnp.exp(math.log(0.03125) - 1.3862944 * jax.random.uniform(streams_of[5], (L, D // 128, R // 128), jnp.float32) ** level_of(streams_of[5], (L, D // 128, R // 128), ((1, 8),), -0.2, 0.2)), 0.0078125, 0.03125),
        "up_codes": scatter_about(streams_of[6], (L, R, D), 1.0, 4.0, ((2, 512),)),
        "up_scales": jnp.clip(jnp.exp(math.log(0.088388346) - 1.3862944 * jax.random.uniform(streams_of[7], (L, R // 128, D // 128), jnp.float32) ** level_of(streams_of[7], (L, R // 128, D // 128), ((2, 8),), -0.2, 0.2)), 0.022097087, 0.088388346),
        "final_gain": jnp.clip(1.0 + 0.15 * jax.random.normal(streams_of[8], (D,), jnp.float32), 0.25, 1.75),
        "head_codes": scatter_about(streams_of[9], (D, V), 1.0, 4.0, ((0, 64), (1, 8))),
        "head_scales": draw_head_scales(jax.random.fold_in(streams_of[11], 71), 0),
    }


eps = 1e-06
tile_edge = 128

def dequant(codes, scales):
    rows_all, cols_all = codes.shape
    blocks = codes.astype(jnp.float32).reshape(rows_all // tile_edge, tile_edge, cols_all // tile_edge, tile_edge)
    blocks = blocks * scales[:, None, :, None]
    return blocks.reshape(rows_all, cols_all).astype(jnp.bfloat16)

def rms_inverse(stream_f):
    return lax.rsqrt(lax.optimization_barrier(jnp.mean(stream_f * stream_f, axis=1)) + eps)

def reference(hidden, targets, lengths, layer_gain, down_codes, down_scales, up_codes, up_scales, final_gain, head_codes, head_scales):
    stream = hidden
    group_width = D // N_TENSOR
    for layer in range(L):
        stream_f = stream.astype(jnp.float32)
        inv = rms_inverse(stream_f)
        normed = (stream_f * inv[:, None] * layer_gain[layer]).astype(jnp.bfloat16).astype(jnp.float32)
        down_weight = dequant(down_codes[layer], down_scales[layer]).astype(jnp.float32)
        latent = jnp.zeros((TOKENS, R), jnp.float32)
        for group in range(N_TENSOR):
            lower = group * group_width
            term = jnp.dot(normed[:, lower:lower + group_width], down_weight[lower:lower + group_width], precision=lax.Precision.HIGHEST)
            term = lax.optimization_barrier(term.astype(jnp.bfloat16))
            latent = latent + term.astype(jnp.float32)
        act = jax.nn.silu(latent).astype(jnp.bfloat16).astype(jnp.float32)
        up_weight = dequant(up_codes[layer], up_scales[layer]).astype(jnp.float32)
        branch = jnp.dot(act, up_weight, precision=lax.Precision.HIGHEST)
        stream = (stream_f + branch).astype(jnp.bfloat16)
    stream_f = stream.astype(jnp.float32)
    inv = rms_inverse(stream_f)
    final = (stream_f * inv[:, None] * final_gain).astype(jnp.bfloat16).astype(jnp.float32)
    head_weight = dequant(head_codes, head_scales).astype(jnp.float32)

    def score(block):
        rows_final, rows_target = block
        logits = jnp.dot(rows_final, head_weight, precision=lax.Precision.HIGHEST)
        top = lax.optimization_barrier(jnp.max(logits, axis=1))
        total = lax.optimization_barrier(jnp.sum(jnp.exp(logits - top[:, None]), axis=1))
        picked = jnp.take_along_axis(logits, rows_target[:, None].astype(jnp.int32), axis=1)[:, 0]
        return picked - (top + jnp.log(total))
    scored = lax.map(score, (final.reshape(N_DP, TOK_DEV, D), targets.reshape(N_DP, TOK_DEV)))
    position = jnp.arange(TOK_DEV, dtype=jnp.int32)
    valid = position[None, :] < lengths[:, None]
    return jnp.where(valid, scored, jnp.zeros_like(scored)).reshape(TOKENS)
```

```python
import jax
import jax.numpy as jnp
from jax import lax
from jax.sharding import PartitionSpec as P

eps = 1e-06
tile_edge = 128
n_x, n_z, n_core = 4, 8, 2
n_y, n_hi = 4, 2
f32 = jnp.float32
bf16 = jnp.bfloat16


def dp_of(x, z, c):
    return (x * n_z + z) * n_core + c


x_groups = [[dp_of(x, z, c) for x in range(n_x)] for z in range(n_z) for c in range(n_core)]
y_groups = [[y * n_hi + h for y in range(n_y)] for h in range(n_hi)]
z_groups = [
    [dp_of(x, z, c) * n_y * n_hi + y * n_hi + h for h in range(n_hi) for z in range(n_z)]
    for x in range(n_x)
    for c in range(n_core)
    for y in range(n_y)
]
core_pairs = [
    (dp_of(x, z, c), dp_of(x, z, 1 - c))
    for x in range(n_x)
    for z in range(n_z)
    for c in range(n_core)
]
hi_pairs = [(y * n_hi + h, y * n_hi + 1 - h) for y in range(n_y) for h in range(n_hi)]


def share(block, axis, groups):
    copies = jnp.broadcast_to(block[None], (len(groups[0]),) + block.shape)
    return lax.all_to_all(copies, axis, 0, 0, axis_index_groups=groups)


def swap_hi(value):
    return lax.ppermute(value, "tensor", hi_pairs)


def in_hi_order(own, peer, hi):
    first = jnp.where(hi == 0, own, peer)
    second = jnp.where(hi == 0, peer, own)
    return first, second


def split_sum(total):
    top = lax.reduce_precision(total, 8, 7)
    return top.astype(bf16), (total - top).astype(bf16)


def silu(value):
    return value / (1.0 + jnp.exp(-value))


def per_device(
    hidden,
    targets,
    lengths,
    layer_gain,
    down_codes,
    down_scales,
    up_codes,
    up_scales,
    final_gain,
    head_codes,
    head_scales,
):
    tok_rows, share_width = hidden.shape
    layers, _, rank = down_codes.shape
    model_width = share_width * n_y * n_hi
    hi = lax.axis_index("tensor") % n_hi
    core = lax.axis_index("dp") % n_core

    with jax.named_scope("head_rows"):
        piece = lax.all_gather(head_codes, "dp", axis=0, tiled=True)

    with jax.named_scope("hidden_hi"):
        hidden_peer = swap_hi(hidden)
        small = jnp.concatenate(
            [layer_gain.reshape(-1), down_scales.reshape(-1), up_scales.reshape(-1)]
        )
        small_peer = swap_hi(small)

    with jax.named_scope("layer_codes"):
        codes = jnp.stack([down_codes, jnp.swapaxes(up_codes, 1, 2)], axis=1)
        rows = codes.shape[2]
        codes = codes.reshape(-1, rank)
        codes = lax.all_gather(
            codes, ("dp", "tensor"), axis=0, tiled=False, axis_index_groups=z_groups
        )
        codes = codes.reshape(-1, rank)
        codes = share(codes, "dp", x_groups)
        other = lax.ppermute(codes, "dp", core_pairs)
        zero, one = jnp.where(core == 0, codes, other), jnp.where(core == 0, other, codes)
        codes = jnp.stack([zero, one])
        codes = codes.reshape(n_core, n_x, n_hi, n_z, layers, 2, rows, rank)
        codes = codes.transpose(4, 5, 2, 1, 3, 0, 6, 7)
        codes = codes.reshape(layers, 2, n_hi * share_width // tile_edge, tile_edge, rank // tile_edge, tile_edge)

    def unpack(flat):
        gain, down, up = jnp.split(flat, [layer_gain.size, layer_gain.size + down_scales.size])
        return (
            gain.reshape(layer_gain.shape),
            down.reshape(down_scales.shape),
            jnp.swapaxes(up.reshape(up_scales.shape), 1, 2),
        )

    flats = in_hi_order(small, small_peer, hi)
    (gain_a, down_a, up_a), (gain_b, down_b, up_b) = unpack(flats[0]), unpack(flats[1])
    gain = jnp.concatenate([gain_a, gain_b], axis=1)
    scales = jnp.stack(
        [jnp.concatenate([down_a, down_b], axis=1), jnp.concatenate([up_a, up_b], axis=1)], axis=1
    )
    weights = codes.astype(f32) * scales[:, :, :, None, :, None]
    weights = weights.astype(bf16).reshape(layers, 2, n_hi * share_width, rank)

    stream = jnp.concatenate(in_hi_order(hidden, hidden_peer, hi), axis=1)
    for layer in range(layers):
        with jax.named_scope("down"):
            stream_f = stream.astype(f32)
            squares = jnp.sum(stream_f * stream_f, axis=1)
            scaled = (stream_f * gain[layer]).astype(bf16)
            part = jnp.dot(scaled, weights[layer, 0], preferred_element_type=f32).astype(bf16)
            top, rest = split_sum(squares)
            extra = jnp.concatenate([top, rest]).reshape(-1, rank)
            extra = jnp.pad(extra, ((0, 16 - extra.shape[0]), (0, 0)))
            parts = share(jnp.concatenate([part, extra], axis=0), "tensor", y_groups)
            parts = jnp.sum(parts.astype(f32), axis=0)
            total = parts[tok_rows:].reshape(-1)
            total = total[:tok_rows] + total[tok_rows : 2 * tok_rows]
        with jax.named_scope("up"):
            inv = lax.rsqrt(total / model_width + eps)
            act = silu(parts[:tok_rows] * inv[:, None]).astype(bf16)
            branch = lax.dot_general(
                act, weights[layer, 1], (((1,), (1,)), ((), ())), preferred_element_type=f32
            )
            stream = (stream_f + branch).astype(bf16)

    with jax.named_scope("stream_y"):
        gathered = share(stream, "tensor", y_groups)
        gathered = jnp.swapaxes(gathered, 0, 1).reshape(tok_rows, model_width)
    with jax.named_scope("head"):
        gathered_f = gathered.astype(f32)
        inv_final = lax.rsqrt(jnp.mean(gathered_f * gathered_f, axis=1) + eps)
        final = (gathered_f * inv_final[:, None] * final_gain).astype(bf16)
        count, local_vocab = piece.shape
        weight = piece.astype(f32).reshape(
            count // tile_edge, tile_edge, local_vocab // tile_edge, tile_edge
        )
        weight = weight * head_scales[:, None, :, None]
        weight = weight.reshape(count, local_vocab).astype(bf16)
        logits = jnp.dot(final, weight, preferred_element_type=f32)
        offset = lax.axis_index("tensor") * local_vocab
        columns = lax.broadcasted_iota(jnp.int32, logits.shape, 1) + offset
        picked = jnp.sum(jnp.where(columns == targets[:, None], logits, 0.0), axis=1)
        top = jnp.max(logits, axis=1)
        total = jnp.sum(jnp.exp(logits - top[:, None]), axis=1)

    def merge(stats):
        tops, totals, picks = stats[:, 0], stats[:, 1], stats[:, 2]
        highest = jnp.max(tops, axis=0)
        total = jnp.sum(totals * jnp.exp(tops - highest), axis=0)
        return jnp.stack([highest, total, jnp.sum(picks, axis=0)])

    with jax.named_scope("stats"):
        mine = merge(share(jnp.stack([top, total, picked]), "tensor", y_groups))
        both = merge(jnp.stack([mine, swap_hi(mine)]))
        scored = both[2] - (both[0] + jnp.log(both[1]))
        position = lax.broadcasted_iota(jnp.int32, (tok_rows,), 0)
        return jnp.where(position < lengths[0], scored, jnp.zeros_like(scored))


def solution(mesh):
    in_specs = (
        P("dp", "tensor"),
        P("dp"),
        P("dp"),
        P(None, "tensor"),
        P(None, ("tensor", "dp"), None),
        P(None, "tensor", None),
        P(None, None, ("tensor", "dp")),
        P(None, None, "tensor"),
        P(),
        P("dp", "tensor"),
        P(None, "tensor"),
    )
    out_specs = P("dp")
    return jax.shard_map(
        per_device, mesh=mesh, in_specs=in_specs, out_specs=out_specs, check_vma=False
    )
```

```python
import functools

import jax
import jax.numpy as jnp
from jax import lax
from jax.experimental import pallas as pl
from jax.experimental.pallas import tpu as pltpu
from jax.sharding import PartitionSpec as P

eps = 1e-06
tile_edge = 128
n_x, n_z, n_core = 4, 8, 2
n_y, n_hi = 4, 2
f32 = jnp.float32
bf16 = jnp.bfloat16
extra_rows = 16
mib = 1 << 20


def dp_of(x, z, c):
    return (x * n_z + z) * n_core + c


x_groups = [[dp_of(x, z, c) for x in range(n_x)] for z in range(n_z) for c in range(n_core)]
y_groups = [[y * n_hi + h for y in range(n_y)] for h in range(n_hi)]
z_groups = [
    [dp_of(x, z, c) * n_y * n_hi + y * n_hi + h for h in range(n_hi) for z in range(n_z)]
    for x in range(n_x)
    for c in range(n_core)
    for y in range(n_y)
]
core_pairs = [
    (dp_of(x, z, c), dp_of(x, z, 1 - c))
    for x in range(n_x)
    for z in range(n_z)
    for c in range(n_core)
]
hi_pairs = [(y * n_hi + h, y * n_hi + 1 - h) for y in range(n_y) for h in range(n_hi)]


def send_alike(copies, axis, groups):
    return lax.all_to_all(copies, axis, 0, 0, axis_index_groups=groups)


def share(block, axis, groups):
    return send_alike(jnp.broadcast_to(block[None], (len(groups[0]),) + block.shape), axis, groups)


def swap_hi(value):
    return lax.ppermute(value, "tensor", hi_pairs)


def swap_core(value):
    return lax.ppermute(value, "dp", core_pairs)


def in_pieces(value):
    high = lax.reduce_precision(value, 8, 7)
    middle = lax.reduce_precision(value - high, 8, 7)
    return jnp.stack([high, middle, value - high - middle]).astype(bf16)


def in_hi_order(own, peer, hi):
    return jnp.where(hi == 0, own, peer), jnp.where(hi == 0, peer, own)


def dot_nt(a, b):
    return lax.dot_general(a, b, (((1,), (1,)), ((), ())), preferred_element_type=f32)


def weight_rows(core, own_ref, other_ref, scale_ref, at, pair):
    blocks = []
    rank = scale_ref.shape[2]
    lanes = pl.ds(at * rank, rank)
    for block in (2 * pair, 2 * pair + 1):
        h, x = divmod(block, n_x)
        rows = pl.ds(h * tile_edge // n_core, tile_edge // n_core)
        own = own_ref[x, rows, lanes].astype(f32)
        other = other_ref[x, rows, lanes].astype(f32)
        zero = jnp.where(core == 0, own, other)
        one = jnp.where(core == 0, other, own)
        cols = own.shape[1]
        both = jnp.concatenate(
            [zero.reshape(n_z, 1, -1, cols), one.reshape(n_z, 1, -1, cols)], axis=1
        ).reshape(tile_edge, cols)
        blocks.append((both * scale_ref[at, pl.ds(block, 1), :]).astype(bf16))
    return jnp.concatenate(blocks, axis=0)


def down_block(stream_block, gain_block, weight):
    values = stream_block.astype(f32)
    part = jnp.dot((values * gain_block).astype(bf16), weight, preferred_element_type=f32)
    square = values * values
    high = square.astype(bf16)
    low = (square - high.astype(f32)).astype(bf16)
    ones = jnp.ones((extra_rows, square.shape[1]), bf16)
    return part, dot_nt(ones, high) + dot_nt(ones, low)


def write_part(out_ref, part, squares):
    tok = part.shape[0]
    high = squares.astype(bf16)
    low = (squares - high.astype(f32)).astype(bf16)
    main = part.astype(bf16)
    rest = jnp.concatenate([high, low], axis=1)
    for y in range(n_y):
        out_ref[y, pl.ds(0, tok), :] = main
        out_ref[y, pl.ds(tok, extra_rows), :] = rest


def read_act(parts_ref, model_width):
    tok = parts_ref.shape[1] - extra_rows
    latent = parts_ref[0, pl.ds(0, tok), :].astype(f32)
    for y in range(1, n_y):
        latent += parts_ref[y, pl.ds(0, tok), :].astype(f32)
    rows = jnp.concatenate(
        [
            parts_ref[y, pl.ds(tok, extra_rows), pl.ds(half * tok, tok)].astype(f32)
            for y in range(n_y)
            for half in range(2)
        ],
        axis=0,
    )
    columns = rows.T.astype(bf16)
    ones = jnp.full((rows.shape[0], latent.shape[1]), 1.0 / extra_rows, bf16)
    total = jnp.dot(columns, ones, preferred_element_type=f32)
    value = latent * lax.rsqrt(total / model_width + eps)
    return (value / (1.0 + jnp.exp(-value))).astype(bf16)


def first_kernel(core_ref, stream_ref, gain_ref, own_ref, other_ref, scale_ref, out_ref):
    core = core_ref[0]
    part, squares = None, None
    for pair in range(stream_ref.shape[1] // (2 * tile_edge)):
        cols = pl.ds(pair * 2 * tile_edge, 2 * tile_edge)
        weight = weight_rows(core, own_ref, other_ref, scale_ref, 0, pair)
        more, more_squares = down_block(stream_ref[:, cols], gain_ref[:, cols], weight)
        part = more if part is None else part + more
        squares = more_squares if squares is None else squares + more_squares
    write_part(out_ref, part, squares)


def middle_kernel(
    core_ref, parts_ref, stream_ref, gain_ref, own_ref, other_ref, scale_ref,
    next_ref, out_ref, *, model_width,
):
    core = core_ref[0]
    act = read_act(parts_ref, model_width)
    part, squares = None, None
    for pair in range(stream_ref.shape[1] // (2 * tile_edge)):
        cols = pl.ds(pair * 2 * tile_edge, 2 * tile_edge)
        up = weight_rows(core, own_ref, other_ref, scale_ref, 1, pair)
        block = (stream_ref[:, cols].astype(f32) + dot_nt(act, up)).astype(bf16)
        next_ref[:, cols] = block
        down = weight_rows(core, own_ref, other_ref, scale_ref, 2, pair)
        more, more_squares = down_block(block, gain_ref[:, cols], down)
        part = more if part is None else part + more
        squares = more_squares if squares is None else squares + more_squares
    write_part(out_ref, part, squares)


def last_kernel(
    core_ref, parts_ref, stream_ref, own_ref, other_ref, scale_ref, out_ref, *, model_width
):
    core = core_ref[0]
    act = read_act(parts_ref, model_width)
    for pair in range(stream_ref.shape[1] // (2 * tile_edge)):
        cols = pl.ds(pair * 2 * tile_edge, 2 * tile_edge)
        up = weight_rows(core, own_ref, other_ref, scale_ref, 3, pair)
        block = (stream_ref[:, cols].astype(f32) + dot_nt(act, up)).astype(bf16)
        for y in range(n_y):
            out_ref[y, :, cols] = block


def head_kernel(
    offset_ref, stream_ref, gain_ref, codes_ref, scale_ref, target_ref, out_ref,
    logits_ref, squares_ref, *, model_width,
):
    step = pl.program_id(0)

    @pl.when(step == 0)
    def _():
        logits_ref[...] = jnp.zeros_like(logits_ref)
        squares_ref[...] = jnp.zeros_like(squares_ref)

    rows = codes_ref.shape[0]
    tok = stream_ref.shape[1]
    vocab = codes_ref.shape[1]
    for part in range(rows // (2 * tile_edge)):
        cols = pl.ds(part * 2 * tile_edge, 2 * tile_edge)
        values = stream_ref[0, :, cols].astype(f32)
        squares_ref[...] += jnp.sum(values * values, axis=1, keepdims=True)
        final = (values * gain_ref[:, cols]).astype(bf16)
        weight = jnp.concatenate(
            [
                (
                    codes_ref[pl.ds(at * tile_edge, tile_edge), :].astype(f32)
                    * scale_ref[at : at + 1, :]
                ).astype(bf16)
                for at in (2 * part, 2 * part + 1)
            ],
            axis=0,
        )
        logits_ref[...] += jnp.dot(final, weight, preferred_element_type=f32)

    @pl.when(step == pl.num_programs(0) - 1)
    def _():
        inv = lax.rsqrt(squares_ref[...] / model_width + eps)
        logits = logits_ref[...] * inv
        columns = lax.broadcasted_iota(jnp.int32, logits.shape, 1) + offset_ref[0]
        picked = jnp.sum(jnp.where(columns == target_ref[...], logits, 0.0), axis=1, keepdims=True)
        top = jnp.max(logits, axis=1, keepdims=True)
        total = jnp.sum(jnp.exp(logits - top), axis=1, keepdims=True)
        lane = lax.broadcasted_iota(jnp.int32, (tok, 128), 1)
        stats = jnp.where(lane == 0, top, jnp.where(lane == 1, total, picked))
        out_ref[...] = stats.T[: out_ref.shape[0], :]


vmem = pl.BlockSpec(memory_space=pltpu.VMEM)
smem = pl.BlockSpec(memory_space=pltpu.SMEM)


def call(kernel, out_shapes, n_operands, flops, **static):
    return pl.pallas_call(
        functools.partial(kernel, **static),
        out_shape=out_shapes,
        in_specs=[smem] + [vmem] * n_operands,
        out_specs=jax.tree.map(lambda _: vmem, out_shapes),
        compiler_params=pltpu.CompilerParams(vmem_limit_bytes=32 * mib),
        cost_estimate=pl.CostEstimate(flops=flops, bytes_accessed=4 * mib, transcendentals=0),
    )


def per_device(
    hidden,
    targets,
    lengths,
    layer_gain,
    down_codes,
    down_scales,
    up_codes,
    up_scales,
    final_gain,
    head_codes,
    head_scales,
):
    tok, share_width = hidden.shape
    layers, rows, rank = down_codes.shape
    assert layers == 2 and rank == 2 * tok
    width = n_hi * share_width
    model_width = share_width * n_y * n_hi
    hi = lax.axis_index("tensor") % n_hi
    core = (lax.axis_index("dp") % n_core).reshape(1)
    local_vocab = head_codes.shape[1]

    with jax.named_scope("head_rows"):
        piece = lax.all_gather(head_codes, "dp", axis=0, tiled=True)

    together = lax.optimization_barrier

    with jax.named_scope("codes_z"):
        codes = jnp.concatenate(
            [down_codes[0], up_codes[0].T, down_codes[1], up_codes[1].T], axis=1
        )
        codes = lax.all_gather(
            codes, ("dp", "tensor"), axis=0, tiled=True, axis_index_groups=z_groups
        )
        hidden, layer_gain, down_scales, up_scales, codes = together(
            (hidden, layer_gain, down_scales, up_scales, codes)
        )

    with jax.named_scope("hidden_hi"):
        small = jnp.concatenate(
            [layer_gain.reshape(-1), down_scales.reshape(-1), up_scales.reshape(-1)]
        )
        small_rows = -(-small.size // rank)
        pieces = jnp.pad(in_pieces(small), ((0, 0), (0, small_rows * rank - small.size)))
        pieces = pieces.reshape(-1, rank)
        pieces = jnp.pad(pieces, ((0, -pieces.shape[0] % extra_rows), (0, 0)))
        peer = swap_hi(jnp.concatenate([hidden, pieces], axis=0))

    with jax.named_scope("codes_x"):
        codes = share(codes, "dp", x_groups)
        codes, peer = together((codes, peer))
        other = swap_core(codes)
        hidden_peer = peer[:tok]
        small_peer = peer[tok : tok + 3 * small_rows].astype(f32).reshape(3, -1).sum(axis=0)
        small_peer = small_peer[: small.size]

    with jax.named_scope("layer_scales"):
        def unpack(flat):
            gain, down, up = jnp.split(
                flat, [layer_gain.size, layer_gain.size + down_scales.size]
            )
            return (
                gain.reshape(layer_gain.shape),
                down.reshape(down_scales.shape),
                jnp.swapaxes(up.reshape(up_scales.shape), 1, 2),
            )

        flats = in_hi_order(small, small_peer, hi)
        (gain_a, down_a, up_a), (gain_b, down_b, up_b) = unpack(flats[0]), unpack(flats[1])
        gain = jnp.concatenate([gain_a, gain_b], axis=1)
        down_s = jnp.concatenate([down_a, down_b], axis=1)
        up_s = jnp.concatenate([up_a, up_b], axis=1)
        scales = jnp.stack([down_s[0], up_s[0], down_s[1], up_s[1]])
        scales = jnp.repeat(scales, tile_edge, axis=2)

    stream = jnp.concatenate(in_hi_order(hidden, hidden_peer, hi), axis=1)
    matmul = 2 * tok * width * rank
    parts_shape = jax.ShapeDtypeStruct((n_y, tok + extra_rows, rank), bf16)
    stream_shape = jax.ShapeDtypeStruct((tok, width), bf16)
    with jax.named_scope("down"):
        parts = call(first_kernel, parts_shape, 5, matmul)(
            core, stream, gain[0:1], codes, other, scales
        )
        parts = send_alike(parts, "tensor", y_groups)
    with jax.named_scope("up_down"):
        stream, parts = call(
            middle_kernel, (stream_shape, parts_shape), 6, 2 * matmul,
            model_width=model_width,
        )(core, parts, stream, gain[1:2], codes, other, scales)
        parts = send_alike(parts, "tensor", y_groups)
    with jax.named_scope("up"):
        stream = call(
            last_kernel, jax.ShapeDtypeStruct((n_y, tok, width), bf16), 5, matmul,
            model_width=model_width,
        )(core, parts, stream, codes, other, scales)
        stream = send_alike(stream, "tensor", y_groups)

    with jax.named_scope("head"):
        offset = (lax.axis_index("tensor") * local_vocab).reshape(1)
        block = 4 * tile_edge
        steps = model_width // block
        per_y = width // block
        stats = pl.pallas_call(
            functools.partial(head_kernel, model_width=model_width),
            out_shape=jax.ShapeDtypeStruct((8, tok), f32),
            grid=(steps,),
            in_specs=[
                smem,
                pl.BlockSpec((1, tok, block), lambda k: (k // per_y, 0, k % per_y)),
                pl.BlockSpec((1, block), lambda k: (0, k)),
                pl.BlockSpec((block, local_vocab), lambda k: (k, 0)),
                pl.BlockSpec((None, block // tile_edge, local_vocab), lambda k: (k, 0, 0)),
                pl.BlockSpec((tok, 1), lambda k: (0, 0)),
            ],
            out_specs=pl.BlockSpec((8, tok), lambda k: (0, 0)),
            scratch_shapes=[pltpu.VMEM((tok, local_vocab), f32), pltpu.VMEM((tok, 1), f32)],
            compiler_params=pltpu.CompilerParams(vmem_limit_bytes=32 * mib),
            cost_estimate=pl.CostEstimate(
                flops=2 * tok * model_width * local_vocab,
                bytes_accessed=2 * model_width * local_vocab,
                transcendentals=0,
            ),
        )(
            offset,
            stream,
            final_gain[None],
            piece,
            jnp.repeat(head_scales, tile_edge, axis=1).reshape(steps, -1, local_vocab),
            targets[:, None],
        )

    def merge(all_stats):
        tops, totals, picks = all_stats[:, 0], all_stats[:, 1], all_stats[:, 2]
        highest = jnp.max(tops, axis=0)
        total = jnp.sum(totals * jnp.exp(tops - highest), axis=0)
        return jnp.stack([highest, total, jnp.sum(picks, axis=0)])

    with jax.named_scope("stats"):
        mine = merge(share(stats[:3], "tensor", y_groups))
        top, total, picked = merge(jnp.stack([mine, swap_hi(mine)]))
        scored = picked - (top + jnp.log(total))
        position = lax.broadcasted_iota(jnp.int32, (tok,), 0)
        return jnp.where(position < lengths[0], scored, jnp.zeros_like(scored))


def solution(mesh):
    in_specs = (
        P("dp", "tensor"),
        P("dp"),
        P("dp"),
        P(None, "tensor"),
        P(None, ("tensor", "dp"), None),
        P(None, "tensor", None),
        P(None, None, ("tensor", "dp")),
        P(None, None, "tensor"),
        P(),
        P("dp", "tensor"),
        P(None, "tensor"),
    )
    out_specs = P("dp")
    return jax.shard_map(
        per_device, mesh=mesh, in_specs=in_specs, out_specs=out_specs, check_vma=False
    )
```

```python
import functools

import jax
import jax.numpy as jnp
from jax import lax
from jax.experimental import pallas as pl
from jax.experimental.pallas import tpu as pltpu
from jax.sharding import PartitionSpec as P

eps = 1e-06
tile_edge = 128
n_x, n_z, n_core = 4, 8, 2
n_y, n_hi = 4, 2
f32 = jnp.float32
bf16 = jnp.bfloat16
extra_rows = 16
mib = 1 << 20


def dp_of(x, z, c):
    return (x * n_z + z) * n_core + c


x_groups = [[dp_of(x, z, c) for x in range(n_x)] for z in range(n_z) for c in range(n_core)]
y_groups = [[y * n_hi + h for y in range(n_y)] for h in range(n_hi)]
z_groups = [
    [dp_of(x, z, c) * n_y * n_hi + y * n_hi + h for h in range(n_hi) for z in range(n_z)]
    for x in range(n_x)
    for c in range(n_core)
    for y in range(n_y)
]
core_pairs = [
    (dp_of(x, z, c), dp_of(x, z, 1 - c))
    for x in range(n_x)
    for z in range(n_z)
    for c in range(n_core)
]
hi_pairs = [(y * n_hi + h, y * n_hi + 1 - h) for y in range(n_y) for h in range(n_hi)]


def send_alike(copies, axis, groups):
    return lax.all_to_all(copies, axis, 0, 0, axis_index_groups=groups)


def share(block, axis, groups):
    return send_alike(jnp.broadcast_to(block[None], (len(groups[0]),) + block.shape), axis, groups)


def swap_hi(value):
    return lax.ppermute(value, "tensor", hi_pairs)


def swap_core(value):
    return lax.ppermute(value, "dp", core_pairs)


def in_pieces(value):
    high = lax.reduce_precision(value, 8, 7)
    middle = lax.reduce_precision(value - high, 8, 7)
    return jnp.stack([high, middle, value - high - middle]).astype(bf16)


def in_hi_order(own, peer, hi):
    return jnp.where(hi == 0, own, peer), jnp.where(hi == 0, peer, own)


def dot_nt(a, b):
    return lax.dot_general(a, b, (((1,), (1,)), ((), ())), preferred_element_type=f32)


def weight_rows(core, own_ref, other_ref, scale_ref, pair):
    blocks = []
    for block in (2 * pair, 2 * pair + 1):
        h, x = divmod(block, n_x)
        rows = pl.ds(h * tile_edge // n_core, tile_edge // n_core)
        own = own_ref[x, rows, :].astype(f32)
        other = other_ref[x, rows, :].astype(f32)
        zero = jnp.where(core == 0, own, other)
        one = jnp.where(core == 0, other, own)
        cols = own.shape[1]
        both = jnp.concatenate(
            [zero.reshape(n_z, 1, -1, cols), one.reshape(n_z, 1, -1, cols)], axis=1
        ).reshape(tile_edge, cols)
        blocks.append((both * scale_ref[0, pl.ds(block, 1), :]).astype(bf16))
    return jnp.concatenate(blocks, axis=0)


def hidden_columns(hi, own_ref, peer_ref, pair):
    h, part = divmod(pair, own_ref.shape[1] // (2 * tile_edge))
    cols = pl.ds(part * 2 * tile_edge, 2 * tile_edge)
    own, peer = own_ref[:, cols].astype(f32), peer_ref[:, cols].astype(f32)
    return jnp.where(hi == h, own, peer)


def down_block(stream_block, gain_block, weight):
    values = stream_block
    part = jnp.dot((values * gain_block).astype(bf16), weight, preferred_element_type=f32)
    square = values * values
    high = square.astype(bf16)
    low = (square - high.astype(f32)).astype(bf16)
    ones = jnp.ones((extra_rows, square.shape[1]), bf16)
    return part, dot_nt(ones, high) + dot_nt(ones, low)


def write_part(out_ref, part, squares):
    tok = part.shape[0]
    high = squares.astype(bf16)
    low = (squares - high.astype(f32)).astype(bf16)
    main = part.astype(bf16)
    rest = jnp.concatenate([high, low], axis=1)
    for y in range(n_y):
        out_ref[y, pl.ds(0, tok), :] = main
        out_ref[y, pl.ds(tok, extra_rows), :] = rest


def read_act(parts_ref, model_width):
    tok = parts_ref.shape[1] - extra_rows
    latent = parts_ref[0, pl.ds(0, tok), :].astype(f32)
    for y in range(1, n_y):
        latent += parts_ref[y, pl.ds(0, tok), :].astype(f32)
    rows = jnp.concatenate(
        [
            parts_ref[y, pl.ds(tok, extra_rows), pl.ds(half * tok, tok)].astype(f32)
            for y in range(n_y)
            for half in range(2)
        ],
        axis=0,
    )
    columns = rows.T.astype(bf16)
    ones = jnp.full((rows.shape[0], latent.shape[1]), 1.0 / extra_rows, bf16)
    total = jnp.dot(columns, ones, preferred_element_type=f32)
    value = latent * lax.rsqrt(total / model_width + eps)
    return (value / (1.0 + jnp.exp(-value))).astype(bf16)


def first_kernel(
    place_ref, hidden_ref, peer_ref, gain_ref, own_ref, other_ref, scale_ref, out_ref
):
    part, squares = 0.0, 0.0
    for pair in range(n_hi * hidden_ref.shape[1] // (2 * tile_edge)):
        cols = pl.ds(pair * 2 * tile_edge, 2 * tile_edge)
        weight = weight_rows(place_ref[0], own_ref, other_ref, scale_ref, pair)
        block = hidden_columns(place_ref[1], hidden_ref, peer_ref, pair)
        more, more_squares = down_block(block, gain_ref[:, cols], weight)
        part, squares = part + more, squares + more_squares
    write_part(out_ref, part, squares)


def middle_kernel(
    place_ref, parts_ref, hidden_ref, peer_ref, gain_ref,
    up_own_ref, up_other_ref, up_scale_ref, down_own_ref, down_other_ref, down_scale_ref,
    next_ref, out_ref, *, model_width,
):
    act = read_act(parts_ref, model_width)
    part, squares = 0.0, 0.0
    for pair in range(n_hi * hidden_ref.shape[1] // (2 * tile_edge)):
        cols = pl.ds(pair * 2 * tile_edge, 2 * tile_edge)
        up = weight_rows(place_ref[0], up_own_ref, up_other_ref, up_scale_ref, pair)
        block = hidden_columns(place_ref[1], hidden_ref, peer_ref, pair)
        block = (block + dot_nt(act, up)).astype(bf16)
        next_ref[:, cols] = block
        down = weight_rows(place_ref[0], down_own_ref, down_other_ref, down_scale_ref, pair)
        more, more_squares = down_block(block.astype(f32), gain_ref[:, cols], down)
        part, squares = part + more, squares + more_squares
    write_part(out_ref, part, squares)


def last_kernel(
    place_ref, parts_ref, stream_ref, own_ref, other_ref, scale_ref, out_ref, *, model_width
):
    act = read_act(parts_ref, model_width)
    for pair in range(stream_ref.shape[1] // (2 * tile_edge)):
        cols = pl.ds(pair * 2 * tile_edge, 2 * tile_edge)
        up = weight_rows(place_ref[0], own_ref, other_ref, scale_ref, pair)
        block = (stream_ref[:, cols].astype(f32) + dot_nt(act, up)).astype(bf16)
        for y in range(n_y):
            out_ref[y, :, cols] = block


def unpack_head_kernel(codes_ref, scale_ref, out_ref):
    for at in range(codes_ref.shape[0] // tile_edge):
        rows = pl.ds(at * tile_edge, tile_edge)
        out_ref[rows, :] = (codes_ref[rows, :].astype(f32) * scale_ref[at : at + 1, :]).astype(bf16)


chunk = 4 * tile_edge


def chunks(width):
    return [pl.ds(at * chunk, chunk) for at in range(width // chunk)]


def head_kernel(offset_ref, stream_ref, gain_ref, weight_ref, target_ref, out_ref, *, model_width):
    tok, width = stream_ref.shape[1:]
    logits, squares = 0.0, 0.0
    for y in range(n_y):
        for cols in chunks(width):
            values = stream_ref[y, :, cols].astype(f32)
            squares = squares + jnp.sum(values * values, axis=1, keepdims=True)
            rows = pl.ds(y * width + cols.start, chunk)
            final = (values * gain_ref[:, rows]).astype(bf16)
            logits = logits + jnp.dot(final, weight_ref[rows, :], preferred_element_type=f32)
    logits = logits * lax.rsqrt(squares / model_width + eps)
    columns = lax.broadcasted_iota(jnp.int32, logits.shape, 1) + offset_ref[0]
    picked = jnp.sum(jnp.where(columns == target_ref[...], logits, 0.0), axis=1, keepdims=True)
    top = jnp.max(logits, axis=1, keepdims=True)
    total = jnp.sum(jnp.exp(logits - top), axis=1, keepdims=True)
    lane = lax.broadcasted_iota(jnp.int32, (tok, 128), 1)
    stats = jnp.where(lane == 0, top, jnp.where(lane == 1, total, picked))
    out_ref[...] = stats.T[: out_ref.shape[0], :]


vmem = pl.BlockSpec(memory_space=pltpu.VMEM)
smem = pl.BlockSpec(memory_space=pltpu.SMEM)


def matrix(at, rank):
    codes = pl.BlockSpec((n_x, n_hi * tile_edge // n_core, rank), lambda i: (0, 0, at))
    return [codes, codes, pl.BlockSpec((1, n_hi * n_x, rank), lambda i: (at, 0, 0))]


def call(kernel, out_shapes, in_specs, flops, steps={"grid": (1,)}, **static):
    return pl.pallas_call(
        functools.partial(kernel, **static),
        out_shape=out_shapes,
        in_specs=[smem] + in_specs,
        out_specs=jax.tree.map(lambda _: vmem, out_shapes),
        compiler_params=pltpu.CompilerParams(vmem_limit_bytes=32 * mib),
        cost_estimate=pl.CostEstimate(flops=flops, bytes_accessed=4 * mib, transcendentals=0),
        **steps,
    )


def per_device(
    hidden,
    targets,
    lengths,
    layer_gain,
    down_codes,
    down_scales,
    up_codes,
    up_scales,
    final_gain,
    head_codes,
    head_scales,
):
    tok, share_width = hidden.shape
    layers, rows, rank = down_codes.shape
    assert layers == 2 and rank == 2 * tok
    width = n_hi * share_width
    model_width = share_width * n_y * n_hi
    hi = lax.axis_index("tensor") % n_hi
    core = (lax.axis_index("dp") % n_core).reshape(1)
    local_vocab = head_codes.shape[1]

    with jax.named_scope("head_rows"):
        piece = lax.all_gather(head_codes, "dp", axis=0, tiled=True)

    together = lax.optimization_barrier

    with jax.named_scope("codes_z"):
        codes = jnp.concatenate(
            [down_codes[0], up_codes[0].T, down_codes[1], up_codes[1].T], axis=1
        )
        codes = lax.all_gather(
            codes, ("dp", "tensor"), axis=0, tiled=True, axis_index_groups=z_groups
        )
        hidden, layer_gain, down_scales, up_scales, codes = together(
            (hidden, layer_gain, down_scales, up_scales, codes)
        )

    with jax.named_scope("hidden_hi"):
        small = jnp.concatenate(
            [layer_gain.reshape(-1), down_scales.reshape(-1), up_scales.reshape(-1)]
        )
        small_rows = -(-small.size // rank)
        pieces = jnp.pad(in_pieces(small), ((0, 0), (0, small_rows * rank - small.size)))
        pieces = pieces.reshape(-1, rank)
        pieces = jnp.pad(pieces, ((0, -pieces.shape[0] % extra_rows), (0, 0)))
        peer = swap_hi(jnp.concatenate([hidden, pieces], axis=0))

    with jax.named_scope("codes_x"):
        codes = share(codes, "dp", x_groups)
        codes, peer = together((codes, peer))
        other = swap_core(codes)
        hidden_peer = peer[:tok]
        small_peer = peer[tok : tok + 3 * small_rows].astype(f32).reshape(3, -1).sum(axis=0)
        small_peer = small_peer[: small.size]

    with jax.named_scope("layer_scales"):
        def unpack(flat):
            gain, down, up = jnp.split(
                flat, [layer_gain.size, layer_gain.size + down_scales.size]
            )
            return (
                gain.reshape(layer_gain.shape),
                down.reshape(down_scales.shape),
                jnp.swapaxes(up.reshape(up_scales.shape), 1, 2),
            )

        flats = in_hi_order(small, small_peer, hi)
        (gain_a, down_a, up_a), (gain_b, down_b, up_b) = unpack(flats[0]), unpack(flats[1])
        gain = jnp.concatenate([gain_a, gain_b], axis=1)
        down_s = jnp.concatenate([down_a, down_b], axis=1)
        up_s = jnp.concatenate([up_a, up_b], axis=1)
        scales = jnp.stack([down_s[0], up_s[0], down_s[1], up_s[1]])
        scales = jnp.repeat(scales, tile_edge, axis=2)

    place = jnp.concatenate([core, hi.reshape(1)])
    matmul = 2 * tok * width * rank
    parts_shape = jax.ShapeDtypeStruct((n_y, tok + extra_rows, rank), bf16)
    stream_shape = jax.ShapeDtypeStruct((tok, width), bf16)
    with jax.named_scope("down"):
        parts = call(first_kernel, parts_shape, [vmem] * 3 + matrix(0, rank), matmul)(
            place, hidden, hidden_peer, gain[0:1], codes, other, scales
        )
        parts = send_alike(parts, "tensor", y_groups)
    with jax.named_scope("up_down"):
        stream, parts = call(
            middle_kernel, (stream_shape, parts_shape),
            [vmem] * 4 + matrix(1, rank) + matrix(2, rank), 2 * matmul, model_width=model_width,
        )(
            place, parts, hidden, hidden_peer, gain[1:2],
            codes, other, scales, codes, other, scales,
        )
        parts = send_alike(parts, "tensor", y_groups)
    with jax.named_scope("up"):
        stream = call(
            last_kernel, jax.ShapeDtypeStruct((n_y, tok, width), bf16),
            [vmem] * 2 + matrix(3, rank), matmul, model_width=model_width,
        )(place, parts, stream, codes, other, scales)
        stream = send_alike(stream, "tensor", y_groups)

    with jax.named_scope("head"):
        offset = (lax.axis_index("tensor") * local_vocab).reshape(1)
        block = 4 * tile_edge
        steps = model_width // block
        weight = pl.pallas_call(
            unpack_head_kernel,
            out_shape=jax.ShapeDtypeStruct(piece.shape, bf16),
            grid=(steps,),
            in_specs=[
                pl.BlockSpec((block, local_vocab), lambda k: (k, 0)),
                pl.BlockSpec((None, block // tile_edge, local_vocab), lambda k: (k, 0, 0)),
            ],
            out_specs=pl.BlockSpec((block, local_vocab), lambda k: (k, 0)),
            compiler_params=pltpu.CompilerParams(vmem_limit_bytes=58 * mib),
            cost_estimate=pl.CostEstimate(
                flops=piece.size, bytes_accessed=4 * piece.size, transcendentals=0
            ),
        )(piece, jnp.repeat(head_scales, tile_edge, axis=1).reshape(steps, -1, local_vocab))
        stats = call(
            head_kernel, jax.ShapeDtypeStruct((8, tok), f32), [vmem] * 4, 2 * tok * model_width * local_vocab,
            steps={}, model_width=model_width,
        )(offset, stream, final_gain[None], weight, targets[:, None])

    def merge(all_stats):
        tops, totals, picks = all_stats[:, 0], all_stats[:, 1], all_stats[:, 2]
        highest = jnp.max(tops, axis=0)
        total = jnp.sum(totals * jnp.exp(tops - highest), axis=0)
        return jnp.stack([highest, total, jnp.sum(picks, axis=0)])

    with jax.named_scope("stats"):
        mine = merge(share(stats[:3], "tensor", y_groups))
        top, total, picked = merge(jnp.stack([mine, swap_hi(mine)]))
        scored = picked - (top + jnp.log(total))
        position = lax.broadcasted_iota(jnp.int32, (tok,), 0)
        return jnp.where(position < lengths[0], scored, jnp.zeros_like(scored))


def solution(mesh):
    in_specs = (
        P("dp", "tensor"),
        P("dp"),
        P("dp"),
        P(None, "tensor"),
        P(None, ("tensor", "dp"), None),
        P(None, "tensor", None),
        P(None, None, ("tensor", "dp")),
        P(None, None, "tensor"),
        P(),
        P("dp", "tensor"),
        P(None, "tensor"),
    )
    out_specs = P("dp")
    return jax.shard_map(
        per_device, mesh=mesh, in_specs=in_specs, out_specs=out_specs, check_vma=False
    )
```

```python
import functools

import jax
import jax.numpy as jnp
from jax import lax
from jax.experimental import pallas as pl
from jax.experimental.pallas import tpu as pltpu
from jax.sharding import PartitionSpec as P

eps = 1e-06
tile_edge = 128
n_x, n_z, n_core = 4, 8, 2
n_y, n_hi = 4, 2
f32 = jnp.float32
bf16 = jnp.bfloat16
extra_rows = 16
mib = 1 << 20


def dp_of(x, z, c):
    return (x * n_z + z) * n_core + c


x_groups = [[dp_of(x, z, c) for x in range(n_x)] for z in range(n_z) for c in range(n_core)]
y_groups = [[y * n_hi + h for y in range(n_y)] for h in range(n_hi)]
z_groups = [
    [dp_of(x, z, c) * n_y * n_hi + y * n_hi + h for h in range(n_hi) for z in range(n_z)]
    for x in range(n_x)
    for c in range(n_core)
    for y in range(n_y)
]
core_pairs = [
    (dp_of(x, z, c), dp_of(x, z, 1 - c))
    for x in range(n_x)
    for z in range(n_z)
    for c in range(n_core)
]
hi_pairs = [(y * n_hi + h, y * n_hi + 1 - h) for y in range(n_y) for h in range(n_hi)]


def send_alike(copies, axis, groups):
    return lax.all_to_all(copies, axis, 0, 0, axis_index_groups=groups)


def share(block, axis, groups):
    return send_alike(jnp.broadcast_to(block[None], (len(groups[0]),) + block.shape), axis, groups)


def swap_hi(value):
    return lax.ppermute(value, "tensor", hi_pairs)


def swap_core(value):
    return lax.ppermute(value, "dp", core_pairs)


def in_pieces(value):
    high = lax.reduce_precision(value, 8, 7)
    middle = lax.reduce_precision(value - high, 8, 7)
    return jnp.stack([high, middle, value - high - middle]).astype(bf16)


def in_hi_order(own, peer, hi):
    return jnp.where(hi == 0, own, peer), jnp.where(hi == 0, peer, own)


def dot_nt(a, b):
    return lax.dot_general(a, b, (((1,), (1,)), ((), ())), preferred_element_type=f32)


def weight_rows(core, own_ref, other_ref, scale_ref, pair):
    blocks = []
    for block in (2 * pair, 2 * pair + 1):
        h, x = divmod(block, n_x)
        rows = pl.ds(h * tile_edge // n_core, tile_edge // n_core)
        own = own_ref[x, rows, :].astype(f32)
        other = other_ref[x, rows, :].astype(f32)
        zero = jnp.where(core == 0, own, other)
        one = jnp.where(core == 0, other, own)
        cols = own.shape[1]
        both = jnp.concatenate(
            [zero.reshape(n_z, 1, -1, cols), one.reshape(n_z, 1, -1, cols)], axis=1
        ).reshape(tile_edge, cols)
        blocks.append((both * scale_ref[0, pl.ds(block, 1), :]).astype(bf16))
    return jnp.concatenate(blocks, axis=0)


def hidden_columns(hi, own_ref, peer_ref, pair):
    h, part = divmod(pair, own_ref.shape[1] // (2 * tile_edge))
    cols = pl.ds(part * 2 * tile_edge, 2 * tile_edge)
    own, peer = own_ref[:, cols].astype(f32), peer_ref[:, cols].astype(f32)
    return jnp.where(hi == h, own, peer)


def down_block(stream_block, gain_block, weight):
    values = stream_block
    part = jnp.dot((values * gain_block).astype(bf16), weight, preferred_element_type=f32)
    square = values * values
    high = square.astype(bf16)
    low = (square - high.astype(f32)).astype(bf16)
    ones = jnp.ones((extra_rows, square.shape[1]), bf16)
    return part, dot_nt(ones, high) + dot_nt(ones, low)


def write_part(out_ref, part, squares):
    tok = part.shape[0]
    high = squares.astype(bf16)
    low = (squares - high.astype(f32)).astype(bf16)
    main = part.astype(bf16)
    rest = jnp.concatenate([high, low], axis=1)
    for y in range(n_y):
        out_ref[y, pl.ds(0, tok), :] = main
        out_ref[y, pl.ds(tok, extra_rows), :] = rest


def read_act(parts_ref, model_width):
    tok = parts_ref.shape[1] - extra_rows
    latent = parts_ref[0, pl.ds(0, tok), :].astype(f32)
    for y in range(1, n_y):
        latent += parts_ref[y, pl.ds(0, tok), :].astype(f32)
    rows = jnp.concatenate(
        [
            parts_ref[y, pl.ds(tok, extra_rows), pl.ds(half * tok, tok)].astype(f32)
            for y in range(n_y)
            for half in range(2)
        ],
        axis=0,
    )
    columns = rows.T.astype(bf16)
    ones = jnp.full((rows.shape[0], latent.shape[1]), 1.0 / extra_rows, bf16)
    total = jnp.dot(columns, ones, preferred_element_type=f32)
    value = latent * lax.rsqrt(total / model_width + eps)
    return (value / (1.0 + jnp.exp(-value))).astype(bf16)


def first_kernel(
    place_ref, hidden_ref, peer_ref, gain_ref, own_ref, other_ref, scale_ref, out_ref
):
    part, squares = 0.0, 0.0
    for pair in range(n_hi * hidden_ref.shape[1] // (2 * tile_edge)):
        cols = pl.ds(pair * 2 * tile_edge, 2 * tile_edge)
        weight = weight_rows(place_ref[0], own_ref, other_ref, scale_ref, pair)
        block = hidden_columns(place_ref[1], hidden_ref, peer_ref, pair)
        more, more_squares = down_block(block, gain_ref[:, cols], weight)
        part, squares = part + more, squares + more_squares
    write_part(out_ref, part, squares)


def middle_kernel(
    place_ref, parts_ref, hidden_ref, peer_ref, gain_ref,
    up_own_ref, up_other_ref, up_scale_ref, down_own_ref, down_other_ref, down_scale_ref,
    next_ref, out_ref, *, model_width,
):
    act = read_act(parts_ref, model_width)
    part, squares = 0.0, 0.0
    for pair in range(n_hi * hidden_ref.shape[1] // (2 * tile_edge)):
        cols = pl.ds(pair * 2 * tile_edge, 2 * tile_edge)
        up = weight_rows(place_ref[0], up_own_ref, up_other_ref, up_scale_ref, pair)
        block = hidden_columns(place_ref[1], hidden_ref, peer_ref, pair)
        block = (block + dot_nt(act, up)).astype(bf16)
        next_ref[:, cols] = block
        down = weight_rows(place_ref[0], down_own_ref, down_other_ref, down_scale_ref, pair)
        more, more_squares = down_block(block.astype(f32), gain_ref[:, cols], down)
        part, squares = part + more, squares + more_squares
    write_part(out_ref, part, squares)


def last_kernel(
    place_ref, parts_ref, stream_ref, own_ref, other_ref, scale_ref, out_ref, *, model_width
):
    act = read_act(parts_ref, model_width)
    for pair in range(stream_ref.shape[1] // (2 * tile_edge)):
        cols = pl.ds(pair * 2 * tile_edge, 2 * tile_edge)
        up = weight_rows(place_ref[0], own_ref, other_ref, scale_ref, pair)
        block = (stream_ref[:, cols].astype(f32) + dot_nt(act, up)).astype(bf16)
        for y in range(n_y):
            out_ref[y, :, cols] = block


def head_kernel(
    offset_ref, stream_ref, gain_ref, codes_ref, scale_ref, target_ref, out_ref,
    logits_ref, squares_ref, *, model_width,
):
    step = pl.program_id(0)

    @pl.when(step == 0)
    def _():
        logits_ref[...] = jnp.zeros_like(logits_ref)
        squares_ref[...] = jnp.zeros_like(squares_ref)

    rows = codes_ref.shape[0]
    tok = stream_ref.shape[1]
    vocab = codes_ref.shape[1]
    for part in range(rows // (2 * tile_edge)):
        cols = pl.ds(part * 2 * tile_edge, 2 * tile_edge)
        values = stream_ref[0, :, cols].astype(f32)
        squares_ref[...] += jnp.sum(values * values, axis=1, keepdims=True)
        final = (values * gain_ref[:, cols]).astype(bf16)
        weight = jnp.concatenate(
            [
                (
                    codes_ref[pl.ds(at * tile_edge, tile_edge), :].astype(f32)
                    * scale_ref[at : at + 1, :]
                ).astype(bf16)
                for at in (2 * part, 2 * part + 1)
            ],
            axis=0,
        )
        logits_ref[...] += jnp.dot(final, weight, preferred_element_type=f32)

    @pl.when(step == pl.num_programs(0) - 1)
    def _():
        inv = lax.rsqrt(squares_ref[...] / model_width + eps)
        logits = logits_ref[...] * inv
        columns = lax.broadcasted_iota(jnp.int32, logits.shape, 1) + offset_ref[0]
        picked = jnp.sum(jnp.where(columns == target_ref[...], logits, 0.0), axis=1, keepdims=True)
        top = jnp.max(logits, axis=1, keepdims=True)
        total = jnp.sum(jnp.exp(logits - top), axis=1, keepdims=True)
        lane = lax.broadcasted_iota(jnp.int32, (tok, 128), 1)
        stats = jnp.where(lane == 0, top, jnp.where(lane == 1, total, picked))
        out_ref[...] = stats.T[: out_ref.shape[0], :]


vmem = pl.BlockSpec(memory_space=pltpu.VMEM)
smem = pl.BlockSpec(memory_space=pltpu.SMEM)


def matrix(at, rank):
    codes = pl.BlockSpec((n_x, n_hi * tile_edge // n_core, rank), lambda i: (0, 0, at))
    return [codes, codes, pl.BlockSpec((1, n_hi * n_x, rank), lambda i: (at, 0, 0))]


def call(kernel, out_shapes, in_specs, flops, **static):
    return pl.pallas_call(
        functools.partial(kernel, **static),
        out_shape=out_shapes,
        grid=(1,),
        in_specs=[smem] + in_specs,
        out_specs=jax.tree.map(lambda _: vmem, out_shapes),
        compiler_params=pltpu.CompilerParams(vmem_limit_bytes=32 * mib),
        cost_estimate=pl.CostEstimate(flops=flops, bytes_accessed=4 * mib, transcendentals=0),
    )


def per_device(
    hidden,
    targets,
    lengths,
    layer_gain,
    down_codes,
    down_scales,
    up_codes,
    up_scales,
    final_gain,
    head_codes,
    head_scales,
):
    tok, share_width = hidden.shape
    layers, rows, rank = down_codes.shape
    assert layers == 2 and rank == 2 * tok
    width = n_hi * share_width
    model_width = share_width * n_y * n_hi
    hi = lax.axis_index("tensor") % n_hi
    core = (lax.axis_index("dp") % n_core).reshape(1)
    local_vocab = head_codes.shape[1]

    with jax.named_scope("head_rows"):
        piece = lax.all_gather(head_codes, "dp", axis=0, tiled=True)

    together = lax.optimization_barrier

    with jax.named_scope("codes_z"):
        codes = jnp.concatenate(
            [down_codes[0], up_codes[0].T, down_codes[1], up_codes[1].T], axis=1
        )
        codes = lax.all_gather(
            codes, ("dp", "tensor"), axis=0, tiled=True, axis_index_groups=z_groups
        )
        hidden, layer_gain, down_scales, up_scales, codes = together(
            (hidden, layer_gain, down_scales, up_scales, codes)
        )

    with jax.named_scope("hidden_hi"):
        small = jnp.concatenate(
            [layer_gain.reshape(-1), down_scales.reshape(-1), up_scales.reshape(-1)]
        )
        small_rows = -(-small.size // rank)
        pieces = jnp.pad(in_pieces(small), ((0, 0), (0, small_rows * rank - small.size)))
        pieces = pieces.reshape(-1, rank)
        pieces = jnp.pad(pieces, ((0, -pieces.shape[0] % extra_rows), (0, 0)))
        peer = swap_hi(jnp.concatenate([hidden, pieces], axis=0))

    with jax.named_scope("codes_x"):
        codes = share(codes, "dp", x_groups)
        codes, peer = together((codes, peer))
        other = swap_core(codes)
        hidden_peer = peer[:tok]
        small_peer = peer[tok : tok + 3 * small_rows].astype(f32).reshape(3, -1).sum(axis=0)
        small_peer = small_peer[: small.size]

    with jax.named_scope("layer_scales"):
        def unpack(flat):
            gain, down, up = jnp.split(
                flat, [layer_gain.size, layer_gain.size + down_scales.size]
            )
            return (
                gain.reshape(layer_gain.shape),
                down.reshape(down_scales.shape),
                jnp.swapaxes(up.reshape(up_scales.shape), 1, 2),
            )

        flats = in_hi_order(small, small_peer, hi)
        (gain_a, down_a, up_a), (gain_b, down_b, up_b) = unpack(flats[0]), unpack(flats[1])
        gain = jnp.concatenate([gain_a, gain_b], axis=1)
        down_s = jnp.concatenate([down_a, down_b], axis=1)
        up_s = jnp.concatenate([up_a, up_b], axis=1)
        scales = jnp.stack([down_s[0], up_s[0], down_s[1], up_s[1]])
        scales = jnp.repeat(scales, tile_edge, axis=2)

    place = jnp.concatenate([core, hi.reshape(1)])
    matmul = 2 * tok * width * rank
    parts_shape = jax.ShapeDtypeStruct((n_y, tok + extra_rows, rank), bf16)
    stream_shape = jax.ShapeDtypeStruct((tok, width), bf16)
    with jax.named_scope("down"):
        parts = call(first_kernel, parts_shape, [vmem] * 3 + matrix(0, rank), matmul)(
            place, hidden, hidden_peer, gain[0:1], codes, other, scales
        )
        parts = send_alike(parts, "tensor", y_groups)
    with jax.named_scope("up_down"):
        stream, parts = call(
            middle_kernel, (stream_shape, parts_shape),
            [vmem] * 4 + matrix(1, rank) + matrix(2, rank), 2 * matmul, model_width=model_width,
        )(
            place, parts, hidden, hidden_peer, gain[1:2],
            codes, other, scales, codes, other, scales,
        )
        parts = send_alike(parts, "tensor", y_groups)
    with jax.named_scope("up"):
        stream = call(
            last_kernel, jax.ShapeDtypeStruct((n_y, tok, width), bf16),
            [vmem] * 2 + matrix(3, rank), matmul, model_width=model_width,
        )(place, parts, stream, codes, other, scales)
        stream = send_alike(stream, "tensor", y_groups)

    with jax.named_scope("head"):
        offset = (lax.axis_index("tensor") * local_vocab).reshape(1)
        block = 4 * tile_edge
        steps = model_width // block
        per_y = width // block
        stats = pl.pallas_call(
            functools.partial(head_kernel, model_width=model_width),
            out_shape=jax.ShapeDtypeStruct((8, tok), f32),
            grid=(steps,),
            in_specs=[
                smem,
                pl.BlockSpec((1, tok, block), lambda k: (k // per_y, 0, k % per_y)),
                pl.BlockSpec((1, block), lambda k: (0, k)),
                pl.BlockSpec((block, local_vocab), lambda k: (k, 0)),
                pl.BlockSpec((None, block // tile_edge, local_vocab), lambda k: (k, 0, 0)),
                pl.BlockSpec((tok, 1), lambda k: (0, 0)),
            ],
            out_specs=pl.BlockSpec((8, tok), lambda k: (0, 0)),
            scratch_shapes=[pltpu.VMEM((tok, local_vocab), f32), pltpu.VMEM((tok, 1), f32)],
            compiler_params=pltpu.CompilerParams(vmem_limit_bytes=32 * mib),
            cost_estimate=pl.CostEstimate(
                flops=2 * tok * model_width * local_vocab,
                bytes_accessed=2 * model_width * local_vocab,
                transcendentals=0,
            ),
        )(
            offset,
            stream,
            final_gain[None],
            piece,
            jnp.repeat(head_scales, tile_edge, axis=1).reshape(steps, -1, local_vocab),
            targets[:, None],
        )

    def merge(all_stats):
        tops, totals, picks = all_stats[:, 0], all_stats[:, 1], all_stats[:, 2]
        highest = jnp.max(tops, axis=0)
        total = jnp.sum(totals * jnp.exp(tops - highest), axis=0)
        return jnp.stack([highest, total, jnp.sum(picks, axis=0)])

    with jax.named_scope("stats"):
        mine = merge(share(stats[:3], "tensor", y_groups))
        top, total, picked = merge(jnp.stack([mine, swap_hi(mine)]))
        scored = picked - (top + jnp.log(total))
        position = lax.broadcasted_iota(jnp.int32, (tok,), 0)
        return jnp.where(position < lengths[0], scored, jnp.zeros_like(scored))


def solution(mesh):
    in_specs = (
        P("dp", "tensor"),
        P("dp"),
        P("dp"),
        P(None, "tensor"),
        P(None, ("tensor", "dp"), None),
        P(None, "tensor", None),
        P(None, None, ("tensor", "dp")),
        P(None, None, "tensor"),
        P(),
        P("dp", "tensor"),
        P(None, "tensor"),
    )
    out_specs = P("dp")
    return jax.shard_map(
        per_device, mesh=mesh, in_specs=in_specs, out_specs=out_specs, check_vma=False
    )
```

```python
import functools

import jax
import jax.numpy as jnp
from jax import lax
from jax.experimental import pallas as pl
from jax.experimental.pallas import tpu as pltpu
from jax.sharding import PartitionSpec as P

eps = 1e-06
tile_edge = 128
n_x, n_z, n_core = 4, 8, 2
n_y, n_hi = 4, 2
f32 = jnp.float32
bf16 = jnp.bfloat16
extra_rows = 16
mib = 1 << 20


def dp_of(x, z, c):
    return (x * n_z + z) * n_core + c


x_groups = [[dp_of(x, z, c) for x in range(n_x)] for z in range(n_z) for c in range(n_core)]
y_groups = [[y * n_hi + h for y in range(n_y)] for h in range(n_hi)]
z_groups = [
    [dp_of(x, z, c) * n_y * n_hi + y * n_hi + h for h in range(n_hi) for z in range(n_z)]
    for x in range(n_x)
    for c in range(n_core)
    for y in range(n_y)
]
core_pairs = [
    (dp_of(x, z, c), dp_of(x, z, 1 - c))
    for x in range(n_x)
    for z in range(n_z)
    for c in range(n_core)
]
hi_pairs = [(y * n_hi + h, y * n_hi + 1 - h) for y in range(n_y) for h in range(n_hi)]


def send_alike(copies, axis, groups):
    return lax.all_to_all(copies, axis, 0, 0, axis_index_groups=groups)


def share(block, axis, groups):
    return send_alike(jnp.broadcast_to(block[None], (len(groups[0]),) + block.shape), axis, groups)


def swap_hi(value):
    return lax.ppermute(value, "tensor", hi_pairs)


def swap_core(value):
    return lax.ppermute(value, "dp", core_pairs)


def in_hi_order(own, peer, hi):
    return jnp.where(hi == 0, own, peer), jnp.where(hi == 0, peer, own)


def dot_nt(a, b):
    return lax.dot_general(a, b, (((1,), (1,)), ((), ())), preferred_element_type=f32)


def weight_rows(core, own_ref, other_ref, scale_ref, pair):
    blocks = []
    for block in (2 * pair, 2 * pair + 1):
        h, x = divmod(block, n_x)
        rows = pl.ds(h * tile_edge // n_core, tile_edge // n_core)
        own = own_ref[x, rows, :].astype(f32)
        other = other_ref[x, rows, :].astype(f32)
        zero = jnp.where(core == 0, own, other)
        one = jnp.where(core == 0, other, own)
        cols = own.shape[1]
        both = jnp.concatenate(
            [zero.reshape(n_z, 1, -1, cols), one.reshape(n_z, 1, -1, cols)], axis=1
        ).reshape(tile_edge, cols)
        blocks.append((both * scale_ref[0, pl.ds(block, 1), :]).astype(bf16))
    return jnp.concatenate(blocks, axis=0)


def hidden_columns(hi, own_ref, peer_ref, pair):
    h, part = divmod(pair, own_ref.shape[1] // (2 * tile_edge))
    cols = pl.ds(part * 2 * tile_edge, 2 * tile_edge)
    own, peer = own_ref[:, cols].astype(f32), peer_ref[:, cols].astype(f32)
    return jnp.where(hi == h, own, peer)


def down_block(stream_block, gain_block, weight):
    values = stream_block
    part = jnp.dot((values * gain_block).astype(bf16), weight, preferred_element_type=f32)
    square = values * values
    high = square.astype(bf16)
    low = (square - high.astype(f32)).astype(bf16)
    ones = jnp.ones((extra_rows, square.shape[1]), bf16)
    return part, dot_nt(ones, high) + dot_nt(ones, low)


def write_part(out_ref, part, squares):
    tok = part.shape[0]
    high = squares.astype(bf16)
    low = (squares - high.astype(f32)).astype(bf16)
    main = part.astype(bf16)
    rest = jnp.concatenate([high, low], axis=1)
    for y in range(n_y):
        out_ref[y, pl.ds(0, tok), :] = main
        out_ref[y, pl.ds(tok, extra_rows), :] = rest


def read_act(parts_ref, model_width):
    tok = parts_ref.shape[1] - extra_rows
    latent = parts_ref[0, pl.ds(0, tok), :].astype(f32)
    for y in range(1, n_y):
        latent += parts_ref[y, pl.ds(0, tok), :].astype(f32)
    rows = jnp.concatenate(
        [
            parts_ref[y, pl.ds(tok, extra_rows), pl.ds(half * tok, tok)].astype(f32)
            for y in range(n_y)
            for half in range(2)
        ],
        axis=0,
    )
    columns = rows.T.astype(bf16)
    ones = jnp.full((rows.shape[0], latent.shape[1]), 1.0 / extra_rows, bf16)
    total = jnp.dot(columns, ones, preferred_element_type=f32)
    value = latent * lax.rsqrt(total / model_width + eps)
    return (value / (1.0 + jnp.exp(-value))).astype(bf16)


def first_kernel(
    place_ref, hidden_ref, peer_ref, gain_ref, own_ref, other_ref, scale_ref, out_ref
):
    part, squares = 0.0, 0.0
    for pair in range(n_hi * hidden_ref.shape[1] // (2 * tile_edge)):
        cols = pl.ds(pair * 2 * tile_edge, 2 * tile_edge)
        weight = weight_rows(place_ref[0], own_ref, other_ref, scale_ref, pair)
        block = hidden_columns(place_ref[1], hidden_ref, peer_ref, pair)
        more, more_squares = down_block(block, gain_ref[:, cols], weight)
        part, squares = part + more, squares + more_squares
    write_part(out_ref, part, squares)


def middle_kernel(
    place_ref, parts_ref, hidden_ref, peer_ref, gain_ref,
    up_own_ref, up_other_ref, up_scale_ref, down_own_ref, down_other_ref, down_scale_ref,
    next_ref, out_ref, *, model_width,
):
    act = read_act(parts_ref, model_width)
    part, squares = 0.0, 0.0
    for pair in range(n_hi * hidden_ref.shape[1] // (2 * tile_edge)):
        cols = pl.ds(pair * 2 * tile_edge, 2 * tile_edge)
        up = weight_rows(place_ref[0], up_own_ref, up_other_ref, up_scale_ref, pair)
        block = hidden_columns(place_ref[1], hidden_ref, peer_ref, pair)
        block = (block + dot_nt(act, up)).astype(bf16)
        next_ref[:, cols] = block
        down = weight_rows(place_ref[0], down_own_ref, down_other_ref, down_scale_ref, pair)
        more, more_squares = down_block(block.astype(f32), gain_ref[:, cols], down)
        part, squares = part + more, squares + more_squares
    write_part(out_ref, part, squares)


def last_kernel(
    place_ref, parts_ref, stream_ref, own_ref, other_ref, scale_ref, out_ref, *, model_width
):
    act = read_act(parts_ref, model_width)
    for pair in range(stream_ref.shape[1] // (2 * tile_edge)):
        cols = pl.ds(pair * 2 * tile_edge, 2 * tile_edge)
        up = weight_rows(place_ref[0], own_ref, other_ref, scale_ref, pair)
        block = (stream_ref[:, cols].astype(f32) + dot_nt(act, up)).astype(bf16)
        for y in range(n_y):
            out_ref[y, :, cols] = block


def head_kernel(
    offset_ref, stream_ref, gain_ref, codes_ref, scale_ref, target_ref, out_ref, *, model_width
):
    n_blocks, tok, width = stream_ref.shape
    chunk = 4 * tile_edge
    logits, squares = 0.0, 0.0
    for at in range(model_width // chunk):
        block, part = divmod(at * chunk, width)
        values = stream_ref[block, :, pl.ds(part, chunk)].astype(f32)
        squares = squares + jnp.sum(values * values, axis=1, keepdims=True)
        final = (values * gain_ref[:, pl.ds(at * chunk, chunk)]).astype(bf16)
        weight = []
        for tile in range(at * chunk // tile_edge, (at + 1) * chunk // tile_edge):
            codes = codes_ref[pl.ds(tile * tile_edge, tile_edge), :].astype(f32)
            weight.append((codes * scale_ref[tile : tile + 1, :]).astype(bf16))
        weight = jnp.concatenate(weight, axis=0)
        logits = logits + jnp.dot(final, weight, preferred_element_type=f32)
    logits = logits * lax.rsqrt(squares / model_width + eps)
    columns = lax.broadcasted_iota(jnp.int32, logits.shape, 1) + offset_ref[0]
    picked = jnp.sum(jnp.where(columns == target_ref[...], logits, 0.0), axis=1, keepdims=True)
    top = jnp.max(logits, axis=1, keepdims=True)
    total = jnp.sum(jnp.exp(logits - top), axis=1, keepdims=True)
    lane = lax.broadcasted_iota(jnp.int32, (tok, 128), 1)
    stats = jnp.where(lane == 0, top, jnp.where(lane == 1, total, picked))
    out_ref[...] = stats.T[: out_ref.shape[0], :]


vmem = pl.BlockSpec(memory_space=pltpu.VMEM)
smem = pl.BlockSpec(memory_space=pltpu.SMEM)


def matrix(at, rank):
    codes = pl.BlockSpec((n_x, n_hi * tile_edge // n_core, rank), lambda i: (0, 0, at))
    return [codes, codes, pl.BlockSpec((1, n_hi * n_x, rank), lambda i: (at, 0, 0))]


def call(kernel, out_shapes, in_specs, flops, **static):
    return pl.pallas_call(
        functools.partial(kernel, **static),
        out_shape=out_shapes,
        grid=(1,),
        in_specs=[smem] + in_specs,
        out_specs=jax.tree.map(lambda _: vmem, out_shapes),
        compiler_params=pltpu.CompilerParams(vmem_limit_bytes=32 * mib),
        cost_estimate=pl.CostEstimate(flops=flops, bytes_accessed=4 * mib, transcendentals=0),
    )


def per_device(
    hidden,
    targets,
    lengths,
    layer_gain,
    down_codes,
    down_scales,
    up_codes,
    up_scales,
    final_gain,
    head_codes,
    head_scales,
):
    tok, share_width = hidden.shape
    layers, rows, rank = down_codes.shape
    assert layers == 2 and rank == 2 * tok
    width = n_hi * share_width
    model_width = share_width * n_y * n_hi
    hi = lax.axis_index("tensor") % n_hi
    core = (lax.axis_index("dp") % n_core).reshape(1)
    local_vocab = head_codes.shape[1]

    with jax.named_scope("head_rows"):
        piece = lax.all_gather(head_codes, "dp", axis=0, tiled=True)

    together = lax.optimization_barrier

    with jax.named_scope("codes_z"):
        codes = jnp.concatenate(
            [down_codes[0], up_codes[0].T, down_codes[1], up_codes[1].T], axis=1
        )
        codes = lax.all_gather(
            codes, ("dp", "tensor"), axis=0, tiled=True, axis_index_groups=z_groups
        )
        hidden, layer_gain, down_scales, up_scales, codes = together(
            (hidden, layer_gain, down_scales, up_scales, codes)
        )

    with jax.named_scope("hidden_hi"):
        hidden_peer = swap_hi(hidden)

    with jax.named_scope("codes_x"):
        codes = share(codes, "dp", x_groups)
        small = jnp.concatenate(
            [layer_gain.reshape(-1), down_scales.reshape(-1), up_scales.reshape(-1)]
        )
        small_peer = swap_hi(small)
        codes, hidden_peer, small_peer = together((codes, hidden_peer, small_peer))
        other = swap_core(codes)

    with jax.named_scope("layer_scales"):
        def unpack(flat):
            gain, down, up = jnp.split(
                flat, [layer_gain.size, layer_gain.size + down_scales.size]
            )
            return (
                gain.reshape(layer_gain.shape),
                down.reshape(down_scales.shape),
                jnp.swapaxes(up.reshape(up_scales.shape), 1, 2),
            )

        flats = in_hi_order(small, small_peer, hi)
        (gain_a, down_a, up_a), (gain_b, down_b, up_b) = unpack(flats[0]), unpack(flats[1])
        gain = jnp.concatenate([gain_a, gain_b], axis=1)
        down_s = jnp.concatenate([down_a, down_b], axis=1)
        up_s = jnp.concatenate([up_a, up_b], axis=1)
        scales = jnp.stack([down_s[0], up_s[0], down_s[1], up_s[1]])
        scales = jnp.repeat(scales, tile_edge, axis=2)

    place = jnp.concatenate([core, hi.reshape(1)])
    matmul = 2 * tok * width * rank
    parts_shape = jax.ShapeDtypeStruct((n_y, tok + extra_rows, rank), bf16)
    stream_shape = jax.ShapeDtypeStruct((tok, width), bf16)
    with jax.named_scope("down"):
        parts = call(first_kernel, parts_shape, [vmem] * 3 + matrix(0, rank), matmul)(
            place, hidden, hidden_peer, gain[0:1], codes, other, scales
        )
        parts = send_alike(parts, "tensor", y_groups)
    with jax.named_scope("up_down"):
        stream, parts = call(
            middle_kernel, (stream_shape, parts_shape),
            [vmem] * 4 + matrix(1, rank) + matrix(2, rank), 2 * matmul, model_width=model_width,
        )(
            place, parts, hidden, hidden_peer, gain[1:2],
            codes, other, scales, codes, other, scales,
        )
        parts = send_alike(parts, "tensor", y_groups)
    with jax.named_scope("up"):
        stream = call(
            last_kernel, jax.ShapeDtypeStruct((n_y, tok, width), bf16),
            [vmem] * 2 + matrix(3, rank), matmul, model_width=model_width,
        )(place, parts, stream, codes, other, scales)
        stream = send_alike(stream, "tensor", y_groups)

    with jax.named_scope("head"):
        offset = (lax.axis_index("tensor") * local_vocab).reshape(1)
        stats = pl.pallas_call(
            functools.partial(head_kernel, model_width=model_width),
            out_shape=jax.ShapeDtypeStruct((8, tok), f32),
            in_specs=[smem] + [vmem] * 5,
            out_specs=vmem,
            compiler_params=pltpu.CompilerParams(vmem_limit_bytes=32 * mib),
            cost_estimate=pl.CostEstimate(
                flops=2 * tok * model_width * local_vocab,
                bytes_accessed=2 * model_width * local_vocab,
                transcendentals=0,
            ),
        )(
            offset,
            stream,
            final_gain[None],
            piece,
            jnp.repeat(head_scales, tile_edge, axis=1),
            targets[:, None],
        )

    def merge(all_stats):
        tops, totals, picks = all_stats[:, 0], all_stats[:, 1], all_stats[:, 2]
        highest = jnp.max(tops, axis=0)
        total = jnp.sum(totals * jnp.exp(tops - highest), axis=0)
        return jnp.stack([highest, total, jnp.sum(picks, axis=0)])

    with jax.named_scope("stats"):
        mine = merge(share(stats[:3], "tensor", y_groups))
        top, total, picked = merge(jnp.stack([mine, swap_hi(mine)]))
        scored = picked - (top + jnp.log(total))
        position = lax.broadcasted_iota(jnp.int32, (tok,), 0)
        return jnp.where(position < lengths[0], scored, jnp.zeros_like(scored))


def solution(mesh):
    in_specs = (
        P("dp", "tensor"),
        P("dp"),
        P("dp"),
        P(None, "tensor"),
        P(None, ("tensor", "dp"), None),
        P(None, "tensor", None),
        P(None, None, ("tensor", "dp")),
        P(None, None, "tensor"),
        P(),
        P("dp", "tensor"),
        P(None, "tensor"),
    )
    out_specs = P("dp")
    return jax.shard_map(
        per_device, mesh=mesh, in_specs=in_specs, out_specs=out_specs, check_vma=False
    )
```

```python
import functools

import jax
import jax.numpy as jnp
from jax import lax
from jax.experimental import pallas as pl
from jax.experimental.pallas import tpu as pltpu
from jax.sharding import PartitionSpec as P

eps = 1e-06
tile_edge = 128
n_x, n_z, n_core = 4, 8, 2
n_y, n_hi = 4, 2
f32 = jnp.float32
bf16 = jnp.bfloat16
extra_rows = 16
mib = 1 << 20


def dp_of(x, z, c):
    return (x * n_z + z) * n_core + c


x_groups = [[dp_of(x, z, c) for x in range(n_x)] for z in range(n_z) for c in range(n_core)]
y_groups = [[y * n_hi + h for y in range(n_y)] for h in range(n_hi)]
z_groups = [
    [dp_of(x, z, c) * n_y * n_hi + y * n_hi + h for h in range(n_hi) for z in range(n_z)]
    for x in range(n_x)
    for c in range(n_core)
    for y in range(n_y)
]
core_pairs = [
    (dp_of(x, z, c), dp_of(x, z, 1 - c))
    for x in range(n_x)
    for z in range(n_z)
    for c in range(n_core)
]
hi_pairs = [(y * n_hi + h, y * n_hi + 1 - h) for y in range(n_y) for h in range(n_hi)]


def send_alike(copies, axis, groups):
    return lax.all_to_all(copies, axis, 0, 0, axis_index_groups=groups)


def share(block, axis, groups):
    return send_alike(jnp.broadcast_to(block[None], (len(groups[0]),) + block.shape), axis, groups)


def swap_hi(value):
    return lax.ppermute(value, "tensor", hi_pairs)


def swap_core(value):
    return lax.ppermute(value, "dp", core_pairs)


def in_hi_order(own, peer, hi):
    return jnp.where(hi == 0, own, peer), jnp.where(hi == 0, peer, own)


def dot_nt(a, b):
    return lax.dot_general(a, b, (((1,), (1,)), ((), ())), preferred_element_type=f32)


def weight_rows(core, own_ref, other_ref, scale_ref, pair):
    blocks = []
    for block in (2 * pair, 2 * pair + 1):
        h, x = divmod(block, n_x)
        rows = pl.ds(h * tile_edge // n_core, tile_edge // n_core)
        own = own_ref[x, rows, :].astype(f32)
        other = other_ref[x, rows, :].astype(f32)
        zero = jnp.where(core == 0, own, other)
        one = jnp.where(core == 0, other, own)
        cols = own.shape[1]
        both = jnp.concatenate(
            [zero.reshape(n_z, 1, -1, cols), one.reshape(n_z, 1, -1, cols)], axis=1
        ).reshape(tile_edge, cols)
        blocks.append((both * scale_ref[0, pl.ds(block, 1), :]).astype(bf16))
    return jnp.concatenate(blocks, axis=0)


def hidden_columns(hi, own_ref, peer_ref, pair):
    h, part = divmod(pair, own_ref.shape[1] // (2 * tile_edge))
    cols = pl.ds(part * 2 * tile_edge, 2 * tile_edge)
    own, peer = own_ref[:, cols].astype(f32), peer_ref[:, cols].astype(f32)
    return jnp.where(hi == h, own, peer)


def down_block(stream_block, gain_block, weight):
    values = stream_block
    part = jnp.dot((values * gain_block).astype(bf16), weight, preferred_element_type=f32)
    square = values * values
    high = square.astype(bf16)
    low = (square - high.astype(f32)).astype(bf16)
    ones = jnp.ones((extra_rows, square.shape[1]), bf16)
    return part, dot_nt(ones, high) + dot_nt(ones, low)


def write_part(out_ref, part, squares):
    tok = part.shape[0]
    high = squares.astype(bf16)
    low = (squares - high.astype(f32)).astype(bf16)
    main = part.astype(bf16)
    rest = jnp.concatenate([high, low], axis=1)
    for y in range(n_y):
        out_ref[y, pl.ds(0, tok), :] = main
        out_ref[y, pl.ds(tok, extra_rows), :] = rest


def read_act(parts_ref, model_width):
    tok = parts_ref.shape[1] - extra_rows
    latent = parts_ref[0, pl.ds(0, tok), :].astype(f32)
    for y in range(1, n_y):
        latent += parts_ref[y, pl.ds(0, tok), :].astype(f32)
    rows = jnp.concatenate(
        [
            parts_ref[y, pl.ds(tok, extra_rows), pl.ds(half * tok, tok)].astype(f32)
            for y in range(n_y)
            for half in range(2)
        ],
        axis=0,
    )
    columns = rows.T.astype(bf16)
    ones = jnp.full((rows.shape[0], latent.shape[1]), 1.0 / extra_rows, bf16)
    total = jnp.dot(columns, ones, preferred_element_type=f32)
    value = latent * lax.rsqrt(total / model_width + eps)
    return (value / (1.0 + jnp.exp(-value))).astype(bf16)


def first_kernel(
    place_ref, hidden_ref, peer_ref, gain_ref, own_ref, other_ref, scale_ref, out_ref
):
    part, squares = 0.0, 0.0
    for pair in range(n_hi * hidden_ref.shape[1] // (2 * tile_edge)):
        cols = pl.ds(pair * 2 * tile_edge, 2 * tile_edge)
        weight = weight_rows(place_ref[0], own_ref, other_ref, scale_ref, pair)
        block = hidden_columns(place_ref[1], hidden_ref, peer_ref, pair)
        more, more_squares = down_block(block, gain_ref[:, cols], weight)
        part, squares = part + more, squares + more_squares
    write_part(out_ref, part, squares)


def middle_kernel(
    place_ref, parts_ref, hidden_ref, peer_ref, gain_ref,
    up_own_ref, up_other_ref, up_scale_ref, down_own_ref, down_other_ref, down_scale_ref,
    next_ref, out_ref, *, model_width,
):
    act = read_act(parts_ref, model_width)
    part, squares = 0.0, 0.0
    for pair in range(n_hi * hidden_ref.shape[1] // (2 * tile_edge)):
        cols = pl.ds(pair * 2 * tile_edge, 2 * tile_edge)
        up = weight_rows(place_ref[0], up_own_ref, up_other_ref, up_scale_ref, pair)
        block = hidden_columns(place_ref[1], hidden_ref, peer_ref, pair)
        block = (block + dot_nt(act, up)).astype(bf16)
        next_ref[:, cols] = block
        down = weight_rows(place_ref[0], down_own_ref, down_other_ref, down_scale_ref, pair)
        more, more_squares = down_block(block.astype(f32), gain_ref[:, cols], down)
        part, squares = part + more, squares + more_squares
    write_part(out_ref, part, squares)


def last_kernel(
    place_ref, parts_ref, stream_ref, own_ref, other_ref, scale_ref, out_ref, *, model_width
):
    act = read_act(parts_ref, model_width)
    for pair in range(stream_ref.shape[1] // (2 * tile_edge)):
        cols = pl.ds(pair * 2 * tile_edge, 2 * tile_edge)
        up = weight_rows(place_ref[0], own_ref, other_ref, scale_ref, pair)
        block = (stream_ref[:, cols].astype(f32) + dot_nt(act, up)).astype(bf16)
        for y in range(n_y):
            out_ref[y, :, cols] = block


def head_kernel(
    offset_ref, stream_ref, gain_ref, codes_ref, scale_ref, target_ref, out_ref, *, model_width
):
    n_blocks, tok, width = stream_ref.shape
    chunk = 4 * tile_edge
    logits, squares = 0.0, 0.0
    for at in range(model_width // chunk):
        block, part = divmod(at * chunk, width)
        values = stream_ref[block, :, pl.ds(part, chunk)].astype(f32)
        squares = squares + jnp.sum(values * values, axis=1, keepdims=True)
        final = (values * gain_ref[:, pl.ds(at * chunk, chunk)]).astype(bf16)
        weight = []
        for tile in range(at * chunk // tile_edge, (at + 1) * chunk // tile_edge):
            codes = codes_ref[pl.ds(tile * tile_edge, tile_edge), :].astype(f32)
            weight.append((codes * scale_ref[tile : tile + 1, :]).astype(bf16))
        weight = jnp.concatenate(weight, axis=0)
        logits = logits + jnp.dot(final, weight, preferred_element_type=f32)
    logits = logits * lax.rsqrt(squares / model_width + eps)
    columns = lax.broadcasted_iota(jnp.int32, logits.shape, 1) + offset_ref[0]
    target = jnp.broadcast_to(target_ref[...].astype(f32), (128, tok)).T[:, :1].astype(jnp.int32)
    picked = jnp.sum(jnp.where(columns == target, logits, 0.0), axis=1, keepdims=True)
    top = jnp.max(logits, axis=1, keepdims=True)
    total = jnp.sum(jnp.exp(logits - top), axis=1, keepdims=True)
    lane = lax.broadcasted_iota(jnp.int32, (tok, 128), 1)
    stats = jnp.where(lane == 0, top, jnp.where(lane == 1, total, picked))
    out_ref[...] = stats.T[: out_ref.shape[0], :]


vmem = pl.BlockSpec(memory_space=pltpu.VMEM)
smem = pl.BlockSpec(memory_space=pltpu.SMEM)


def matrix(at, rank):
    codes = pl.BlockSpec((n_x, n_hi * tile_edge // n_core, rank), lambda i: (0, 0, at))
    return [codes, codes, pl.BlockSpec((1, n_hi * n_x, rank), lambda i: (at, 0, 0))]


def call(kernel, out_shapes, in_specs, flops, **static):
    return pl.pallas_call(
        functools.partial(kernel, **static),
        out_shape=out_shapes,
        grid=(1,),
        in_specs=[smem] + in_specs,
        out_specs=jax.tree.map(lambda _: vmem, out_shapes),
        compiler_params=pltpu.CompilerParams(vmem_limit_bytes=32 * mib),
        cost_estimate=pl.CostEstimate(flops=flops, bytes_accessed=4 * mib, transcendentals=0),
    )


def per_device(
    hidden,
    targets,
    lengths,
    layer_gain,
    down_codes,
    down_scales,
    up_codes,
    up_scales,
    final_gain,
    head_codes,
    head_scales,
):
    tok, share_width = hidden.shape
    layers, rows, rank = down_codes.shape
    assert layers == 2 and rank == 2 * tok
    width = n_hi * share_width
    model_width = share_width * n_y * n_hi
    hi = lax.axis_index("tensor") % n_hi
    core = (lax.axis_index("dp") % n_core).reshape(1)
    local_vocab = head_codes.shape[1]

    with jax.named_scope("head_rows"):
        piece = lax.all_gather(head_codes, "dp", axis=0, tiled=True)

    together = lax.optimization_barrier

    with jax.named_scope("codes_z"):
        codes = jnp.stack([down_codes, jnp.swapaxes(up_codes, 1, 2)], axis=1)
        codes = codes.reshape(-1, rank)
        codes = lax.all_gather(
            codes, ("dp", "tensor"), axis=0, tiled=True, axis_index_groups=z_groups
        )
        hidden, layer_gain, down_scales, up_scales, codes = together(
            (hidden, layer_gain, down_scales, up_scales, codes)
        )

    with jax.named_scope("hidden_hi"):
        hidden_peer = swap_hi(hidden)

    with jax.named_scope("codes_x"):
        codes = codes.reshape(n_hi * n_z, 2 * layers, rows, rank).swapaxes(1, 2)
        codes = share(codes.reshape(-1, 2 * layers * rank), "dp", x_groups)
        small = jnp.concatenate(
            [layer_gain.reshape(-1), down_scales.reshape(-1), up_scales.reshape(-1)]
        )
        small_peer = swap_hi(small)
        target_row = targets[None]
        head_rows = jnp.repeat(head_scales, tile_edge, axis=1)
        offset = (lax.axis_index("tensor") * local_vocab).reshape(1)
        final_row = final_gain[None]
        codes, hidden_peer, small_peer, target_row, head_rows, offset, final_row = together(
            (codes, hidden_peer, small_peer, target_row, head_rows, offset, final_row)
        )
        other = swap_core(codes)

    with jax.named_scope("layer_scales"):
        def unpack(flat):
            gain, down, up = jnp.split(
                flat, [layer_gain.size, layer_gain.size + down_scales.size]
            )
            return (
                gain.reshape(layer_gain.shape),
                down.reshape(down_scales.shape),
                jnp.swapaxes(up.reshape(up_scales.shape), 1, 2),
            )

        flats = in_hi_order(small, small_peer, hi)
        (gain_a, down_a, up_a), (gain_b, down_b, up_b) = unpack(flats[0]), unpack(flats[1])
        gain = jnp.concatenate([gain_a, gain_b], axis=1)
        down_s = jnp.concatenate([down_a, down_b], axis=1)
        up_s = jnp.concatenate([up_a, up_b], axis=1)
        scales = jnp.stack([down_s[0], up_s[0], down_s[1], up_s[1]])
        scales = jnp.repeat(scales, tile_edge, axis=2)

    place = jnp.concatenate([core, hi.reshape(1)])
    matmul = 2 * tok * width * rank
    parts_shape = jax.ShapeDtypeStruct((n_y, tok + extra_rows, rank), bf16)
    stream_shape = jax.ShapeDtypeStruct((tok, width), bf16)
    with jax.named_scope("down"):
        parts = call(first_kernel, parts_shape, [vmem] * 3 + matrix(0, rank), matmul)(
            place, hidden, hidden_peer, gain[0:1], codes, other, scales
        )
        parts = send_alike(parts, "tensor", y_groups)
    with jax.named_scope("up_down"):
        stream, parts = call(
            middle_kernel, (stream_shape, parts_shape),
            [vmem] * 4 + matrix(1, rank) + matrix(2, rank), 2 * matmul, model_width=model_width,
        )(
            place, parts, hidden, hidden_peer, gain[1:2],
            codes, other, scales, codes, other, scales,
        )
        parts = send_alike(parts, "tensor", y_groups)
    with jax.named_scope("up"):
        stream = call(
            last_kernel, jax.ShapeDtypeStruct((n_y, tok, width), bf16),
            [vmem] * 2 + matrix(3, rank), matmul, model_width=model_width,
        )(place, parts, stream, codes, other, scales)
        stream = send_alike(stream, "tensor", y_groups)

    with jax.named_scope("head"):
        stats = pl.pallas_call(
            functools.partial(head_kernel, model_width=model_width),
            out_shape=jax.ShapeDtypeStruct((8, tok), f32),
            in_specs=[smem] + [vmem] * 5,
            out_specs=vmem,
            compiler_params=pltpu.CompilerParams(vmem_limit_bytes=32 * mib),
            cost_estimate=pl.CostEstimate(
                flops=2 * tok * model_width * local_vocab,
                bytes_accessed=2 * model_width * local_vocab,
                transcendentals=0,
            ),
        )(
            offset,
            stream,
            final_row,
            piece,
            head_rows,
            target_row,
        )

    def merge(all_stats):
        tops, totals, picks = all_stats[:, 0], all_stats[:, 1], all_stats[:, 2]
        highest = jnp.max(tops, axis=0)
        total = jnp.sum(totals * jnp.exp(tops - highest), axis=0)
        return jnp.stack([highest, total, jnp.sum(picks, axis=0)])

    with jax.named_scope("stats"):
        mine = merge(share(stats[:3], "tensor", y_groups))
        top, total, picked = merge(jnp.stack([mine, swap_hi(mine)]))
        scored = picked - (top + jnp.log(total))
        position = lax.broadcasted_iota(jnp.int32, (tok,), 0)
        return jnp.where(position < lengths[0], scored, jnp.zeros_like(scored))


def solution(mesh):
    in_specs = (
        P("dp", "tensor"),
        P("dp"),
        P("dp"),
        P(None, "tensor"),
        P(None, ("tensor", "dp"), None),
        P(None, "tensor", None),
        P(None, None, ("tensor", "dp")),
        P(None, None, "tensor"),
        P(),
        P("dp", "tensor"),
        P(None, "tensor"),
    )
    out_specs = P("dp")
    return jax.shard_map(
        per_device, mesh=mesh, in_specs=in_specs, out_specs=out_specs, check_vma=False
    )
```

```python
import functools

import jax
import jax.numpy as jnp
from jax import lax
from jax.experimental import pallas as pl
from jax.experimental.pallas import tpu as pltpu
from jax.sharding import PartitionSpec as P

eps = 1e-06
tile_edge = 128
n_x, n_z, n_core = 4, 8, 2
n_y, n_hi = 4, 2
f32 = jnp.float32
bf16 = jnp.bfloat16
extra_rows = 16
mib = 1 << 20


def dp_of(x, z, c):
    return (x * n_z + z) * n_core + c


x_groups = [[dp_of(x, z, c) for x in range(n_x)] for z in range(n_z) for c in range(n_core)]
sum_groups = [[y * n_hi + h for y in (0, 2, 1, 3)] for h in range(n_hi)]
y_groups = [[y * n_hi + h for y in range(n_y)] for h in range(n_hi)]
z_groups = [
    [dp_of(x, z, c) * n_y * n_hi + y * n_hi + h for h in range(n_hi) for z in range(n_z)]
    for x in range(n_x)
    for c in range(n_core)
    for y in range(n_y)
]
core_pairs = [
    (dp_of(x, z, c), dp_of(x, z, 1 - c))
    for x in range(n_x)
    for z in range(n_z)
    for c in range(n_core)
]
hi_pairs = [(y * n_hi + h, y * n_hi + 1 - h) for y in range(n_y) for h in range(n_hi)]


def send_alike(copies, axis, groups):
    return lax.all_to_all(copies, axis, 0, 0, axis_index_groups=groups)


def share(block, axis, groups):
    return send_alike(jnp.broadcast_to(block[None], (len(groups[0]),) + block.shape), axis, groups)


def swap_hi(value):
    return lax.ppermute(value, "tensor", hi_pairs)


def swap_core(value):
    return lax.ppermute(value, "dp", core_pairs)


def in_hi_order(own, peer, hi):
    return jnp.where(hi == 0, own, peer), jnp.where(hi == 0, peer, own)


def dot_nt(a, b):
    return lax.dot_general(a, b, (((1,), (1,)), ((), ())), preferred_element_type=f32)


def weight_rows(core, own_ref, other_ref, scale_ref, pair):
    blocks = []
    for block in (2 * pair, 2 * pair + 1):
        h, x = divmod(block, n_x)
        rows = pl.ds(h * tile_edge // n_core, tile_edge // n_core)
        own = own_ref[x, rows, :].astype(f32)
        other = other_ref[x, rows, :].astype(f32)
        zero = jnp.where(core == 0, own, other)
        one = jnp.where(core == 0, other, own)
        cols = own.shape[1]
        both = jnp.concatenate(
            [zero.reshape(n_z, 1, -1, cols), one.reshape(n_z, 1, -1, cols)], axis=1
        ).reshape(tile_edge, cols)
        blocks.append((both * scale_ref[0, pl.ds(block, 1), :]).astype(bf16))
    return jnp.concatenate(blocks, axis=0)


def hidden_columns(hi, own_ref, peer_ref, pair):
    h, part = divmod(pair, own_ref.shape[1] // (2 * tile_edge))
    cols = pl.ds(part * 2 * tile_edge, 2 * tile_edge)
    own, peer = own_ref[:, cols].astype(f32), peer_ref[:, cols].astype(f32)
    return jnp.where(hi == h, own, peer)


def down_block(stream_block, gain_block, weight):
    values = stream_block
    part = jnp.dot((values * gain_block).astype(bf16), weight, preferred_element_type=f32)
    square = values * values
    high = square.astype(bf16)
    low = (square - high.astype(f32)).astype(bf16)
    ones = jnp.ones((extra_rows, square.shape[1]), bf16)
    return part, dot_nt(ones, high) + dot_nt(ones, low)


def write_part(out_ref, part, squares):
    tok = part.shape[0]
    high = squares.astype(bf16)
    low = (squares - high.astype(f32)).astype(bf16)
    main = part.astype(bf16)
    rest = jnp.concatenate([high, low], axis=1)
    for y in range(n_y):
        out_ref[y, pl.ds(0, tok), :] = main
        out_ref[y, pl.ds(tok, extra_rows), :] = rest


def read_act(parts_ref, model_width):
    tok = parts_ref.shape[1] - extra_rows
    latent = parts_ref[0, pl.ds(0, tok), :].astype(f32)
    for y in range(1, n_y):
        latent += parts_ref[y, pl.ds(0, tok), :].astype(f32)
    rows = jnp.concatenate(
        [
            parts_ref[y, pl.ds(tok, extra_rows), pl.ds(half * tok, tok)].astype(f32)
            for y in range(n_y)
            for half in range(2)
        ],
        axis=0,
    )
    columns = rows.T.astype(bf16)
    ones = jnp.full((rows.shape[0], latent.shape[1]), 1.0 / extra_rows, bf16)
    total = jnp.dot(columns, ones, preferred_element_type=f32)
    value = latent * lax.rsqrt(total / model_width + eps)
    return (value / (1.0 + jnp.exp(-value))).astype(bf16)


def first_kernel(
    place_ref, hidden_ref, peer_ref, gain_ref, own_ref, other_ref, scale_ref, out_ref
):
    part, squares = 0.0, 0.0
    for pair in range(n_hi * hidden_ref.shape[1] // (2 * tile_edge)):
        cols = pl.ds(pair * 2 * tile_edge, 2 * tile_edge)
        weight = weight_rows(place_ref[0], own_ref, other_ref, scale_ref, pair)
        block = hidden_columns(place_ref[1], hidden_ref, peer_ref, pair)
        more, more_squares = down_block(block, gain_ref[:, cols], weight)
        part, squares = part + more, squares + more_squares
    write_part(out_ref, part, squares)


def middle_kernel(
    place_ref, parts_ref, hidden_ref, peer_ref, gain_ref,
    up_own_ref, up_other_ref, up_scale_ref, down_own_ref, down_other_ref, down_scale_ref,
    next_ref, out_ref, *, model_width,
):
    act = read_act(parts_ref, model_width)
    part, squares = 0.0, 0.0
    for pair in range(n_hi * hidden_ref.shape[1] // (2 * tile_edge)):
        cols = pl.ds(pair * 2 * tile_edge, 2 * tile_edge)
        up = weight_rows(place_ref[0], up_own_ref, up_other_ref, up_scale_ref, pair)
        block = hidden_columns(place_ref[1], hidden_ref, peer_ref, pair)
        block = (block + dot_nt(act, up)).astype(bf16)
        next_ref[:, cols] = block
        down = weight_rows(place_ref[0], down_own_ref, down_other_ref, down_scale_ref, pair)
        more, more_squares = down_block(block.astype(f32), gain_ref[:, cols], down)
        part, squares = part + more, squares + more_squares
    write_part(out_ref, part, squares)


def last_kernel(
    place_ref, parts_ref, stream_ref, own_ref, other_ref, scale_ref, out_ref, *, model_width
):
    act = read_act(parts_ref, model_width)
    for pair in range(stream_ref.shape[1] // (2 * tile_edge)):
        cols = pl.ds(pair * 2 * tile_edge, 2 * tile_edge)
        up = weight_rows(place_ref[0], own_ref, other_ref, scale_ref, pair)
        block = (stream_ref[:, cols].astype(f32) + dot_nt(act, up)).astype(bf16)
        for y in range(n_y):
            out_ref[y, :, cols] = block


def head_kernel(
    offset_ref, stream_ref, gain_ref, codes_ref, scale_ref, target_ref, out_ref, *, model_width
):
    n_blocks, tok, width = stream_ref.shape
    chunk = 4 * tile_edge
    logits, squares = 0.0, 0.0
    for at in range(model_width // chunk):
        block, part = divmod(at * chunk, width)
        values = stream_ref[block, :, pl.ds(part, chunk)].astype(f32)
        squares = squares + jnp.sum(values * values, axis=1, keepdims=True)
        final = (values * gain_ref[:, pl.ds(at * chunk, chunk)]).astype(bf16)
        weight = []
        for tile in range(at * chunk // tile_edge, (at + 1) * chunk // tile_edge):
            codes = codes_ref[pl.ds(tile * tile_edge, tile_edge), :].astype(f32)
            weight.append((codes * scale_ref[tile : tile + 1, :]).astype(bf16))
        weight = jnp.concatenate(weight, axis=0)
        logits = logits + jnp.dot(final, weight, preferred_element_type=f32)
    logits = logits * lax.rsqrt(squares / model_width + eps)
    columns = lax.broadcasted_iota(jnp.int32, logits.shape, 1) + offset_ref[0]
    target = jnp.broadcast_to(target_ref[...].astype(f32), (128, tok)).T[:, :1].astype(jnp.int32)
    picked = jnp.sum(jnp.where(columns == target, logits, 0.0), axis=1, keepdims=True)
    top = jnp.max(logits, axis=1, keepdims=True)
    total = jnp.sum(jnp.exp(logits - top), axis=1, keepdims=True)
    lane = lax.broadcasted_iota(jnp.int32, (tok, 128), 1)
    stats = jnp.where(lane == 0, top, jnp.where(lane == 1, total, picked))
    out_ref[...] = stats.T[: out_ref.shape[0], :]


vmem = pl.BlockSpec(memory_space=pltpu.VMEM)
smem = pl.BlockSpec(memory_space=pltpu.SMEM)


def matrix(at, rank):
    codes = pl.BlockSpec((n_x, n_hi * tile_edge // n_core, rank), lambda i: (0, 0, at))
    return [codes, codes, pl.BlockSpec((1, n_hi * n_x, rank), lambda i: (at, 0, 0))]


def call(kernel, out_shapes, in_specs, flops, **static):
    return pl.pallas_call(
        functools.partial(kernel, **static),
        out_shape=out_shapes,
        grid=(1,),
        in_specs=[smem] + in_specs,
        out_specs=jax.tree.map(lambda _: vmem, out_shapes),
        compiler_params=pltpu.CompilerParams(vmem_limit_bytes=32 * mib),
        cost_estimate=pl.CostEstimate(flops=flops, bytes_accessed=4 * mib, transcendentals=0),
    )


def per_device(
    hidden,
    targets,
    lengths,
    layer_gain,
    down_codes,
    down_scales,
    up_codes,
    up_scales,
    final_gain,
    head_codes,
    head_scales,
):
    tok, share_width = hidden.shape
    layers, rows, rank = down_codes.shape
    assert layers == 2 and rank == 2 * tok
    width = n_hi * share_width
    model_width = share_width * n_y * n_hi
    hi = lax.axis_index("tensor") % n_hi
    core = (lax.axis_index("dp") % n_core).reshape(1)
    local_vocab = head_codes.shape[1]

    with jax.named_scope("head_rows"):
        piece = lax.all_gather(head_codes, "dp", axis=0, tiled=True)

    together = lax.optimization_barrier

    with jax.named_scope("codes_z"):
        codes = jnp.stack([down_codes, jnp.swapaxes(up_codes, 1, 2)], axis=1)
        codes = codes.reshape(-1, rank)
        codes = lax.all_gather(
            codes, ("dp", "tensor"), axis=0, tiled=True, axis_index_groups=z_groups
        )
        hidden, layer_gain, down_scales, up_scales, codes = together(
            (hidden, layer_gain, down_scales, up_scales, codes)
        )

    with jax.named_scope("hidden_hi"):
        hidden_peer = swap_hi(hidden)

    with jax.named_scope("codes_x"):
        codes = codes.reshape(n_hi * n_z, 2 * layers, rows, rank).swapaxes(1, 2)
        codes = share(codes.reshape(-1, 2 * layers * rank), "dp", x_groups)
        small = jnp.concatenate(
            [layer_gain.reshape(-1), down_scales.reshape(-1), up_scales.reshape(-1)]
        )
        small_peer = swap_hi(small)
        target_row = targets[None]
        head_rows = jnp.repeat(head_scales, tile_edge, axis=1)
        offset = (lax.axis_index("tensor") * local_vocab).reshape(1)
        final_row = final_gain[None]
        codes, hidden_peer, small_peer, target_row, head_rows, offset, final_row = together(
            (codes, hidden_peer, small_peer, target_row, head_rows, offset, final_row)
        )
        other = swap_core(codes)

    with jax.named_scope("layer_scales"):
        def unpack(flat):
            gain, down, up = jnp.split(
                flat, [layer_gain.size, layer_gain.size + down_scales.size]
            )
            return (
                gain.reshape(layer_gain.shape),
                down.reshape(down_scales.shape),
                jnp.swapaxes(up.reshape(up_scales.shape), 1, 2),
            )

        flats = in_hi_order(small, small_peer, hi)
        (gain_a, down_a, up_a), (gain_b, down_b, up_b) = unpack(flats[0]), unpack(flats[1])
        gain = jnp.concatenate([gain_a, gain_b], axis=1)
        down_s = jnp.concatenate([down_a, down_b], axis=1)
        up_s = jnp.concatenate([up_a, up_b], axis=1)
        scales = jnp.stack([down_s[0], up_s[0], down_s[1], up_s[1]])
        scales = jnp.repeat(scales, tile_edge, axis=2)

    place = jnp.concatenate([core, hi.reshape(1)])
    matmul = 2 * tok * width * rank
    parts_shape = jax.ShapeDtypeStruct((n_y, tok + extra_rows, rank), bf16)
    stream_shape = jax.ShapeDtypeStruct((tok, width), bf16)
    with jax.named_scope("down"):
        parts = call(first_kernel, parts_shape, [vmem] * 3 + matrix(0, rank), matmul)(
            place, hidden, hidden_peer, gain[0:1], codes, other, scales
        )
        parts = send_alike(parts, "tensor", sum_groups)
    with jax.named_scope("up_down"):
        stream, parts = call(
            middle_kernel, (stream_shape, parts_shape),
            [vmem] * 4 + matrix(1, rank) + matrix(2, rank), 2 * matmul, model_width=model_width,
        )(
            place, parts, hidden, hidden_peer, gain[1:2],
            codes, other, scales, codes, other, scales,
        )
        parts = send_alike(parts, "tensor", sum_groups)
    with jax.named_scope("up"):
        stream = call(
            last_kernel, jax.ShapeDtypeStruct((n_y, tok, width), bf16),
            [vmem] * 2 + matrix(3, rank), matmul, model_width=model_width,
        )(place, parts, stream, codes, other, scales)
        stream = send_alike(stream, "tensor", y_groups)

    with jax.named_scope("head"):
        stats = pl.pallas_call(
            functools.partial(head_kernel, model_width=model_width),
            out_shape=jax.ShapeDtypeStruct((8, tok), f32),
            in_specs=[smem] + [vmem] * 5,
            out_specs=vmem,
            compiler_params=pltpu.CompilerParams(vmem_limit_bytes=32 * mib),
            cost_estimate=pl.CostEstimate(
                flops=2 * tok * model_width * local_vocab,
                bytes_accessed=2 * model_width * local_vocab,
                transcendentals=0,
            ),
        )(
            offset,
            stream,
            final_row,
            piece,
            head_rows,
            target_row,
        )

    def merge(all_stats):
        tops, totals, picks = all_stats[:, 0], all_stats[:, 1], all_stats[:, 2]
        highest = jnp.max(tops, axis=0)
        total = jnp.sum(totals * jnp.exp(tops - highest), axis=0)
        return jnp.stack([highest, total, jnp.sum(picks, axis=0)])

    with jax.named_scope("stats"):
        mine = merge(share(stats[:3], "tensor", y_groups))
        top, total, picked = merge(jnp.stack([mine, swap_hi(mine)]))
        scored = picked - (top + jnp.log(total))
        position = lax.broadcasted_iota(jnp.int32, (tok,), 0)
        return jnp.where(position < lengths[0], scored, jnp.zeros_like(scored))


def solution(mesh):
    in_specs = (
        P("dp", "tensor"),
        P("dp"),
        P("dp"),
        P(None, "tensor"),
        P(None, ("tensor", "dp"), None),
        P(None, "tensor", None),
        P(None, None, ("tensor", "dp")),
        P(None, None, "tensor"),
        P(),
        P("dp", "tensor"),
        P(None, "tensor"),
    )
    out_specs = P("dp")
    return jax.shard_map(
        per_device, mesh=mesh, in_specs=in_specs, out_specs=out_specs, check_vma=False
    )
```

```python
import functools

import jax
import jax.numpy as jnp
from jax import lax
from jax.experimental import pallas as pl
from jax.experimental.pallas import tpu as pltpu
from jax.sharding import PartitionSpec as P

eps = 1e-06
tile_edge = 128
n_x, n_z, n_core = 4, 8, 2
n_y, n_hi = 4, 2
f32 = jnp.float32
bf16 = jnp.bfloat16
extra_rows = 16
mib = 1 << 20


def dp_of(x, z, c):
    return (x * n_z + z) * n_core + c


x_groups = [[dp_of(x, z, c) for x in range(n_x)] for z in range(n_z) for c in range(n_core)]
y_order = (0, 2, 1, 3)
y_groups = [[y * n_hi + h for y in y_order] for h in range(n_hi)]
z_groups = [
    [dp_of(x, z, c) * n_y * n_hi + y * n_hi + h for h in range(n_hi) for z in range(n_z)]
    for x in range(n_x)
    for c in range(n_core)
    for y in range(n_y)
]
core_pairs = [
    (dp_of(x, z, c), dp_of(x, z, 1 - c))
    for x in range(n_x)
    for z in range(n_z)
    for c in range(n_core)
]
hi_pairs = [(y * n_hi + h, y * n_hi + 1 - h) for y in range(n_y) for h in range(n_hi)]


def send_alike(copies, axis, groups):
    return lax.all_to_all(copies, axis, 0, 0, axis_index_groups=groups)


def share(block, axis, groups):
    return send_alike(jnp.broadcast_to(block[None], (len(groups[0]),) + block.shape), axis, groups)


def swap_hi(value):
    return lax.ppermute(value, "tensor", hi_pairs)


def swap_core(value):
    return lax.ppermute(value, "dp", core_pairs)


def in_hi_order(own, peer, hi):
    return jnp.where(hi == 0, own, peer), jnp.where(hi == 0, peer, own)


def dot_nt(a, b):
    return lax.dot_general(a, b, (((1,), (1,)), ((), ())), preferred_element_type=f32)


def weight_rows(core, own_ref, other_ref, scale_ref, pair):
    blocks = []
    for block in (2 * pair, 2 * pair + 1):
        h, x = divmod(block, n_x)
        rows = pl.ds(h * tile_edge // n_core, tile_edge // n_core)
        own = own_ref[x, rows, :].astype(f32)
        other = other_ref[x, rows, :].astype(f32)
        zero = jnp.where(core == 0, own, other)
        one = jnp.where(core == 0, other, own)
        cols = own.shape[1]
        both = jnp.concatenate(
            [zero.reshape(n_z, 1, -1, cols), one.reshape(n_z, 1, -1, cols)], axis=1
        ).reshape(tile_edge, cols)
        blocks.append((both * scale_ref[0, pl.ds(block, 1), :]).astype(bf16))
    return jnp.concatenate(blocks, axis=0)


def hidden_columns(hi, own_ref, peer_ref, pair):
    h, part = divmod(pair, own_ref.shape[1] // (2 * tile_edge))
    cols = pl.ds(part * 2 * tile_edge, 2 * tile_edge)
    own, peer = own_ref[:, cols].astype(f32), peer_ref[:, cols].astype(f32)
    return jnp.where(hi == h, own, peer)


def down_block(stream_block, gain_block, weight):
    values = stream_block
    part = jnp.dot((values * gain_block).astype(bf16), weight, preferred_element_type=f32)
    square = values * values
    high = square.astype(bf16)
    low = (square - high.astype(f32)).astype(bf16)
    ones = jnp.ones((extra_rows, square.shape[1]), bf16)
    return part, dot_nt(ones, high) + dot_nt(ones, low)


def write_part(out_ref, part, squares):
    tok = part.shape[0]
    high = squares.astype(bf16)
    low = (squares - high.astype(f32)).astype(bf16)
    main = part.astype(bf16)
    rest = jnp.concatenate([high, low], axis=1)
    for y in range(n_y):
        out_ref[y, pl.ds(0, tok), :] = main
        out_ref[y, pl.ds(tok, extra_rows), :] = rest


def read_act(parts_ref, model_width):
    tok = parts_ref.shape[1] - extra_rows
    latent = parts_ref[0, pl.ds(0, tok), :].astype(f32)
    for y in range(1, n_y):
        latent += parts_ref[y, pl.ds(0, tok), :].astype(f32)
    rows = jnp.concatenate(
        [
            parts_ref[y, pl.ds(tok, extra_rows), pl.ds(half * tok, tok)].astype(f32)
            for y in range(n_y)
            for half in range(2)
        ],
        axis=0,
    )
    columns = rows.T.astype(bf16)
    ones = jnp.full((rows.shape[0], latent.shape[1]), 1.0 / extra_rows, bf16)
    total = jnp.dot(columns, ones, preferred_element_type=f32)
    value = latent * lax.rsqrt(total / model_width + eps)
    return (value / (1.0 + jnp.exp(-value))).astype(bf16)


def first_kernel(
    place_ref, hidden_ref, peer_ref, gain_ref, own_ref, other_ref, scale_ref, out_ref
):
    part, squares = 0.0, 0.0
    for pair in range(n_hi * hidden_ref.shape[1] // (2 * tile_edge)):
        cols = pl.ds(pair * 2 * tile_edge, 2 * tile_edge)
        weight = weight_rows(place_ref[0], own_ref, other_ref, scale_ref, pair)
        block = hidden_columns(place_ref[1], hidden_ref, peer_ref, pair)
        more, more_squares = down_block(block, gain_ref[:, cols], weight)
        part, squares = part + more, squares + more_squares
    write_part(out_ref, part, squares)


def middle_kernel(
    place_ref, parts_ref, hidden_ref, peer_ref, gain_ref,
    up_own_ref, up_other_ref, up_scale_ref, down_own_ref, down_other_ref, down_scale_ref,
    next_ref, out_ref, *, model_width,
):
    act = read_act(parts_ref, model_width)
    part, squares = 0.0, 0.0
    for pair in range(n_hi * hidden_ref.shape[1] // (2 * tile_edge)):
        cols = pl.ds(pair * 2 * tile_edge, 2 * tile_edge)
        up = weight_rows(place_ref[0], up_own_ref, up_other_ref, up_scale_ref, pair)
        block = hidden_columns(place_ref[1], hidden_ref, peer_ref, pair)
        block = (block + dot_nt(act, up)).astype(bf16)
        next_ref[:, cols] = block
        down = weight_rows(place_ref[0], down_own_ref, down_other_ref, down_scale_ref, pair)
        more, more_squares = down_block(block.astype(f32), gain_ref[:, cols], down)
        part, squares = part + more, squares + more_squares
    write_part(out_ref, part, squares)


def last_kernel(
    place_ref, parts_ref, stream_ref, own_ref, other_ref, scale_ref, out_ref, *, model_width
):
    act = read_act(parts_ref, model_width)
    for pair in range(stream_ref.shape[1] // (2 * tile_edge)):
        cols = pl.ds(pair * 2 * tile_edge, 2 * tile_edge)
        up = weight_rows(place_ref[0], own_ref, other_ref, scale_ref, pair)
        block = (stream_ref[:, cols].astype(f32) + dot_nt(act, up)).astype(bf16)
        for y in range(n_y):
            out_ref[y, :, cols] = block


def head_kernel(
    offset_ref, stream_ref, gain_ref, codes_ref, scale_ref, target_ref, out_ref, *, model_width
):
    n_blocks, tok, width = stream_ref.shape
    chunk = 4 * tile_edge
    logits, squares = 0.0, 0.0
    for at in range(model_width // chunk):
        block, part = divmod(at * chunk, width)
        values = stream_ref[y_order[block], :, pl.ds(part, chunk)].astype(f32)
        squares = squares + jnp.sum(values * values, axis=1, keepdims=True)
        final = (values * gain_ref[:, pl.ds(at * chunk, chunk)]).astype(bf16)
        weight = []
        for tile in range(at * chunk // tile_edge, (at + 1) * chunk // tile_edge):
            codes = codes_ref[pl.ds(tile * tile_edge, tile_edge), :].astype(f32)
            weight.append((codes * scale_ref[tile : tile + 1, :]).astype(bf16))
        weight = jnp.concatenate(weight, axis=0)
        logits = logits + jnp.dot(final, weight, preferred_element_type=f32)
    logits = logits * lax.rsqrt(squares / model_width + eps)
    columns = lax.broadcasted_iota(jnp.int32, logits.shape, 1) + offset_ref[0]
    target = jnp.broadcast_to(target_ref[...].astype(f32), (128, tok)).T[:, :1].astype(jnp.int32)
    picked = jnp.sum(jnp.where(columns == target, logits, 0.0), axis=1, keepdims=True)
    top = jnp.max(logits, axis=1, keepdims=True)
    total = jnp.sum(jnp.exp(logits - top), axis=1, keepdims=True)
    lane = lax.broadcasted_iota(jnp.int32, (tok, 128), 1)
    stats = jnp.where(lane == 0, top, jnp.where(lane == 1, total, picked))
    out_ref[...] = stats.T[: out_ref.shape[0], :]


vmem = pl.BlockSpec(memory_space=pltpu.VMEM)
smem = pl.BlockSpec(memory_space=pltpu.SMEM)


def matrix(at, rank):
    codes = pl.BlockSpec((n_x, n_hi * tile_edge // n_core, rank), lambda i: (0, 0, at))
    return [codes, codes, pl.BlockSpec((1, n_hi * n_x, rank), lambda i: (at, 0, 0))]


def call(kernel, out_shapes, in_specs, flops, **static):
    return pl.pallas_call(
        functools.partial(kernel, **static),
        out_shape=out_shapes,
        grid=(1,),
        in_specs=[smem] + in_specs,
        out_specs=jax.tree.map(lambda _: vmem, out_shapes),
        compiler_params=pltpu.CompilerParams(vmem_limit_bytes=32 * mib),
        cost_estimate=pl.CostEstimate(flops=flops, bytes_accessed=4 * mib, transcendentals=0),
    )


def per_device(
    hidden,
    targets,
    lengths,
    layer_gain,
    down_codes,
    down_scales,
    up_codes,
    up_scales,
    final_gain,
    head_codes,
    head_scales,
):
    tok, share_width = hidden.shape
    layers, rows, rank = down_codes.shape
    assert layers == 2 and rank == 2 * tok
    width = n_hi * share_width
    model_width = share_width * n_y * n_hi
    hi = lax.axis_index("tensor") % n_hi
    core = (lax.axis_index("dp") % n_core).reshape(1)
    local_vocab = head_codes.shape[1]

    with jax.named_scope("head_rows"):
        piece = lax.all_gather(head_codes, "dp", axis=0, tiled=True)

    together = lax.optimization_barrier

    with jax.named_scope("codes_z"):
        codes = jnp.stack([down_codes, jnp.swapaxes(up_codes, 1, 2)], axis=1)
        codes = codes.reshape(-1, rank)
        codes = lax.all_gather(
            codes, ("dp", "tensor"), axis=0, tiled=True, axis_index_groups=z_groups
        )
        hidden, layer_gain, down_scales, up_scales, codes = together(
            (hidden, layer_gain, down_scales, up_scales, codes)
        )

    with jax.named_scope("hidden_hi"):
        hidden_peer = swap_hi(hidden)

    with jax.named_scope("codes_x"):
        codes = codes.reshape(n_hi * n_z, 2 * layers, rows, rank).swapaxes(1, 2)
        codes = share(codes.reshape(-1, 2 * layers * rank), "dp", x_groups)
        small = jnp.concatenate(
            [layer_gain.reshape(-1), down_scales.reshape(-1), up_scales.reshape(-1)]
        )
        small_peer = swap_hi(small)
        target_row = targets[None]
        head_rows = jnp.repeat(head_scales, tile_edge, axis=1)
        offset = (lax.axis_index("tensor") * local_vocab).reshape(1)
        final_row = final_gain[None]
        codes, hidden_peer, small_peer, target_row, head_rows, offset, final_row = together(
            (codes, hidden_peer, small_peer, target_row, head_rows, offset, final_row)
        )
        other = swap_core(codes)

    with jax.named_scope("layer_scales"):
        def unpack(flat):
            gain, down, up = jnp.split(
                flat, [layer_gain.size, layer_gain.size + down_scales.size]
            )
            return (
                gain.reshape(layer_gain.shape),
                down.reshape(down_scales.shape),
                jnp.swapaxes(up.reshape(up_scales.shape), 1, 2),
            )

        flats = in_hi_order(small, small_peer, hi)
        (gain_a, down_a, up_a), (gain_b, down_b, up_b) = unpack(flats[0]), unpack(flats[1])
        gain = jnp.concatenate([gain_a, gain_b], axis=1)
        down_s = jnp.concatenate([down_a, down_b], axis=1)
        up_s = jnp.concatenate([up_a, up_b], axis=1)
        scales = jnp.stack([down_s[0], up_s[0], down_s[1], up_s[1]])
        scales = jnp.repeat(scales, tile_edge, axis=2)

    place = jnp.concatenate([core, hi.reshape(1)])
    matmul = 2 * tok * width * rank
    parts_shape = jax.ShapeDtypeStruct((n_y, tok + extra_rows, rank), bf16)
    stream_shape = jax.ShapeDtypeStruct((tok, width), bf16)
    with jax.named_scope("down"):
        parts = call(first_kernel, parts_shape, [vmem] * 3 + matrix(0, rank), matmul)(
            place, hidden, hidden_peer, gain[0:1], codes, other, scales
        )
        parts = send_alike(parts, "tensor", y_groups)
    with jax.named_scope("up_down"):
        stream, parts = call(
            middle_kernel, (stream_shape, parts_shape),
            [vmem] * 4 + matrix(1, rank) + matrix(2, rank), 2 * matmul, model_width=model_width,
        )(
            place, parts, hidden, hidden_peer, gain[1:2],
            codes, other, scales, codes, other, scales,
        )
        parts = send_alike(parts, "tensor", y_groups)
    with jax.named_scope("up"):
        stream = call(
            last_kernel, jax.ShapeDtypeStruct((n_y, tok, width), bf16),
            [vmem] * 2 + matrix(3, rank), matmul, model_width=model_width,
        )(place, parts, stream, codes, other, scales)
        stream = send_alike(stream, "tensor", y_groups)

    with jax.named_scope("head"):
        stats = pl.pallas_call(
            functools.partial(head_kernel, model_width=model_width),
            out_shape=jax.ShapeDtypeStruct((8, tok), f32),
            in_specs=[smem] + [vmem] * 5,
            out_specs=vmem,
            compiler_params=pltpu.CompilerParams(vmem_limit_bytes=32 * mib),
            cost_estimate=pl.CostEstimate(
                flops=2 * tok * model_width * local_vocab,
                bytes_accessed=2 * model_width * local_vocab,
                transcendentals=0,
            ),
        )(
            offset,
            stream,
            final_row,
            piece,
            head_rows,
            target_row,
        )

    def merge(all_stats):
        tops, totals, picks = all_stats[:, 0], all_stats[:, 1], all_stats[:, 2]
        highest = jnp.max(tops, axis=0)
        total = jnp.sum(totals * jnp.exp(tops - highest), axis=0)
        return jnp.stack([highest, total, jnp.sum(picks, axis=0)])

    with jax.named_scope("stats"):
        mine = merge(share(stats[:3], "tensor", y_groups))
        top, total, picked = merge(jnp.stack([mine, swap_hi(mine)]))
        scored = picked - (top + jnp.log(total))
        position = lax.broadcasted_iota(jnp.int32, (tok,), 0)
        return jnp.where(position < lengths[0], scored, jnp.zeros_like(scored))


def solution(mesh):
    in_specs = (
        P("dp", "tensor"),
        P("dp"),
        P("dp"),
        P(None, "tensor"),
        P(None, ("tensor", "dp"), None),
        P(None, "tensor", None),
        P(None, None, ("tensor", "dp")),
        P(None, None, "tensor"),
        P(),
        P("dp", "tensor"),
        P(None, "tensor"),
    )
    out_specs = P("dp")
    return jax.shard_map(
        per_device, mesh=mesh, in_specs=in_specs, out_specs=out_specs, check_vma=False
    )
```
